32 devices in a mesh: cfg: 2 (over y), prow: 8 (over z, x), pcol: 2 (over core).
Axes of the slice: x: 2, y: 2, z: 4, core: 2. Of those that a mesh axis runs over, the one named last changes fastest.
Arguments:
- sigma_top: float32 [2048, 1024], P(('cfg', 'prow'), 'pcol'), parts along dimension 0, as said below
- panel_l: float32 [2048, 4096], P(('cfg', 'pcol'), 'prow'), parts along dimension 0, may hold values from -0.4 to 0.4
- diag_inv: float32 [32, 256, 256], P(('cfg', 'prow')), parts along dimension 0, may hold values from -0.375 to 0.375
- pattern: int32 [32, 8], P(('cfg', 'prow')), parts along dimension 0, may hold values 0 or 1
Outputs:
- sigma_panel: float32 [2048, 4096], P(('cfg', 'pcol'), 'prow'), parts along dimension 0
- sigma_diag: float32 [32, 256, 256], P(('cfg', 'prow')), parts along dimension 0
The draws below stay inside these ranges and needn't reach their ends.
There are 2 independent parts, one for each index of `cfg`. The reference program is written for one: setup_inputs(seed, part) draws one part's arguments, and reference() takes and returns one part's arrays. A program takes and returns all parts, laid end to end along the dimension named above; each array names one. Nothing has to cross between parts.
Inputs may be any that keep to these rules, and one draw needn't show every extreme that they name: sigma_top is symmetric.
All inputs are finite; a program needn't handle non-finite values. No bound on the sum of `pattern` on one device may be relied on, other than what follows from the above.
Results may differ from the reference program's by a relative error of at most 0.000078.
Values sent between devices are 32-bit elements; how exact they have to be, the bound alone decides.
No kernel may reach another device: no remote copies, remote signals or barrier semaphores. Data moves between devices by JAX's collectives and lax.ppermute only.
A program may use at most 64 MiB of HBM per device.

```python
import math
import jax
import jax.numpy as jnp
from jax import lax

W = 1024
SNW = 256
BR = 128
NSN = 16
NCOL = 4096


def draw_sigma_top(key, part):
    key = jax.random.fold_in(key, 11)
    first_key, second_key = jax.random.split(key)
    noise = jax.random.normal(first_key, (W, W), jnp.float32)
    scales = jnp.exp(jax.random.uniform(second_key, (W,), jnp.float32, 0.0, math.log(10.0)))
    symmetric = (noise + jnp.transpose(noise)) * (0.35 / math.sqrt(W))
    root_scale = jnp.sqrt(scales)
    return root_scale[:, None] * (2.0 * jnp.eye(W, dtype=jnp.float32) + symmetric) * root_scale[None, :]


def set_ends(entries, stream_key, least, largest):
    shape = entries.shape
    spot = [jax.random.randint(jax.random.fold_in(stream_key, axis), (), 0, shape[axis]) for axis in range(len(shape))]
    entries = entries.at[tuple(spot)].set(least)
    longest = shape.index(max(shape))
    spot[longest] = (spot[longest] + 1) % shape[longest]
    return entries.at[tuple(spot)].set(largest)


def shard_levels(rng, dims, shards, smallest, high):
    level = 1.0
    for position, shards_of in shards:
        heights = jax.random.uniform(jax.random.fold_in(jax.random.fold_in(rng, 6), position), (shards_of,), jnp.float32, smallest / len(shards), high / len(shards))
        level = level * jnp.repeat(jnp.exp(heights), dims[position] // shards_of).reshape((-1,) + (1,) * (len(dims) - 1 - position))
    return level


def scatter_about(stream_key, dims, width, most, cuts=(), held_as=jnp.bfloat16):
    drawn = jax.random.normal(stream_key, dims, jnp.float32) * width
    if len(cuts) > 0:
        drawn = shard_levels(stream_key, dims, cuts, -0.22, 0.18) * drawn
    return jnp.clip(drawn, min=-most, max=most).astype(held_as)


def setup_inputs(seed: int = 0, part: int = 0) -> dict:
    keys = jax.random.split(jax.random.key(seed), 5)
    own_keys = jax.random.split(jax.random.fold_in(keys[4], part), 5)
    sigma_top = draw_sigma_top(jax.random.fold_in(jax.random.fold_in(keys[4], part), 71), part)
    panel_l = scatter_about(own_keys[1], (W, NCOL), 0.05, 0.4, ((0, 2), (1, 8)), jnp.float32)
    diag_inv = scatter_about(own_keys[2], (NSN, SNW, SNW), SNW ** -0.5, 0.375, ((0, 8),), jnp.float32)
    pattern = set_ends((jax.random.randint(own_keys[3], (NSN, 8), 0, 4) < 3).astype(jnp.int32), jax.random.fold_in(own_keys[3], 1), 0, 1)
    return {"sigma_top": sigma_top, "panel_l": panel_l, "diag_inv": diag_inv, "pattern": pattern}


def reference(sigma_top, panel_l, diag_inv, pattern):
    row_mask = jnp.repeat(pattern.astype(jnp.float32), BR, axis=1)
    panel_three = panel_l.reshape(W, NSN, SNW) * jnp.transpose(row_mask)[:, :, None]
    factor = jnp.einsum("wns,nst->wnt", panel_three, diag_inv, precision=lax.Precision.HIGHEST)
    sigma_three = -jnp.einsum("vw,wnt->vnt", sigma_top, factor, precision=lax.Precision.HIGHEST)
    own_part = jnp.einsum("nsr,nst->nrt", diag_inv, diag_inv, precision=lax.Precision.HIGHEST)
    cross_part = jnp.einsum("wnr,wnt->nrt", factor, sigma_three, precision=lax.Precision.HIGHEST)
    return sigma_three.reshape(W, NCOL), own_part - cross_part
```

```python
import functools

import jax
import jax.numpy as jnp
from jax import lax
from jax.experimental import pallas as pl
from jax.experimental.pallas import tpu as pltpu
from jax.sharding import PartitionSpec as P

W = 1024
BLOCK_ROWS = 8
AXES = ("cfg", "prow", "pcol")
VMEM = pl.BlockSpec(memory_space=pltpu.VMEM)
SMEM = pl.BlockSpec(memory_space=pltpu.SMEM)


def split(value):
    high = value.astype(jnp.bfloat16)
    low = (value - high.astype(jnp.float32)).astype(jnp.bfloat16)
    return high, low


def product(left, right, dims):
    dot = functools.partial(lax.dot_general, dimension_numbers=(dims, ((), ())), preferred_element_type=jnp.float32)
    return dot(left[0], right[0]) + (dot(left[0], right[1]) + dot(left[1], right[0]))


PLAIN = ((1,), (0,))
FIRST = ((0,), (0,))


def factor_kernel(pattern, panel, diag_inv, factor, own_part):
    core = lax.axis_index("pcol")
    rows, width = panel.shape[0], diag_inv.shape[1]
    block = W // BLOCK_ROWS
    for j in range(diag_inv.shape[0]):
        columns = pl.ds(j * width, width)
        inverse = split(diag_inv[j])
        masked = jnp.concatenate(
            [
                panel[pl.ds(r * block, block), columns]
                * pattern[j, core * (rows // block) + r].astype(jnp.float32)
                for r in range(rows // block)
            ],
            axis=0,
        )
        factor[:, columns] = product(split(masked), inverse, PLAIN)
        own_part[j] = product(inverse, inverse, FIRST)


def half_kernel(own, first, second, third, factor, factor_other, gathered, partial):
    prow = lax.axis_index("prow")
    place = lax.rem(prow, 4)
    diagonal = lax.div(prow, 4) == lax.axis_index("pcol")
    rows = own.shape[0]
    x_place = place + 1 - 2 * lax.rem(place, 2)
    z_place = lax.rem(place + 2, 4)
    both = lax.rem(x_place + 2, 4)
    for value, at in (
        (own, place),
        (first, jnp.where(diagonal, z_place, x_place)),
        (second, jnp.where(diagonal, x_place, z_place)),
        (third, both),
    ):
        gathered[pl.ds(pl.multiple_of(at * rows, rows), rows), :] = value[...]

    @pl.when(diagonal)
    def _():
        partial[...] = product(split(gathered[...]), split(factor[...]), FIRST)

    @pl.when(jnp.logical_not(diagonal))
    def _():
        partial[...] = product(split(gathered[...]), split(factor_other[...]), FIRST)


def panel_kernel(near_z, near_x, far_z, far_x, beside, partial, factor, factor_other, sigma, cross, block):
    prow = lax.axis_index("prow")
    place = lax.rem(prow, 4)
    diagonal = lax.div(prow, 4) == lax.axis_index("pcol")
    rows = near_z.shape[0]
    x_place = place + 1 - 2 * lax.rem(place, 2)
    z_place = lax.rem(place + 2, 4)
    both = lax.rem(x_place + 2, 4)
    own_factor = split(factor[...])

    @pl.when(diagonal)
    def _():
        sigma[...] = -(partial[...] + product(split(beside[...]), split(factor_other[...]), PLAIN))

    @pl.when(jnp.logical_not(diagonal))
    def _():
        for value, at in ((near_z, place), (near_x, x_place), (far_z, z_place), (far_x, both)):
            block[pl.ds(pl.multiple_of(at * rows, rows), rows), :] = value[...]
        sigma[...] = -(partial[...] + product(split(block[...]), own_factor, PLAIN))

    width = cross.shape[1]
    sigma_split = split(sigma[...])
    for j in range(cross.shape[0]):
        columns = slice(j * width, (j + 1) * width)
        cross[j] = product(
            tuple(part[:, columns] for part in own_factor), tuple(part[:, columns] for part in sigma_split), FIRST
        )


def call(kernel, out_shapes, flops, *args, smem=0, scratch=()):
    moved = sum(a.size * 4 for a in args) + sum(4 * o.size for o in out_shapes)
    return pl.pallas_call(
        kernel,
        out_shape=out_shapes,
        in_specs=[SMEM] * smem + [VMEM] * (len(args) - smem),
        out_specs=[VMEM] * len(out_shapes),
        scratch_shapes=scratch,
        cost_estimate=pl.CostEstimate(flops=flops, bytes_accessed=moved, transcendentals=0),
        compiler_params=pltpu.CompilerParams(vmem_limit_bytes=32 * 1024 * 1024),
    )(*args)


def permute(value, mesh, diagonal_step, other_step, swap=False):
    cfgs, prows, cores = (mesh.shape[axis] for axis in AXES)
    pairs = []
    for c in range(cfgs):
        for p in range(prows):
            for k in range(cores):
                step = diagonal_step if (p >= prows // 2) == (k == 1) else other_step
                if step is None:
                    continue
                to = 1 - k if swap else k
                pairs.append(((c * prows + p) * cores + k, (c * prows + (p ^ step)) * cores + to))
    return lax.ppermute(value, AXES, pairs)


def local_eight(mesh, sigma_top, panel_l, diag_inv, pattern):
    f32 = jnp.float32
    half_rows, own_columns = panel_l.shape
    shape = lambda *dims: jax.ShapeDtypeStruct(dims, f32)
    first = permute(sigma_top, mesh, 2, 1)
    near_z = permute(sigma_top, mesh, 4, None)
    far_z = permute(sigma_top, mesh, 6, None)
    second = permute(sigma_top, mesh, 1, 2)
    factor, own_part = call(
        factor_kernel,
        [shape(half_rows, own_columns), shape(*diag_inv.shape)],
        2 * half_rows * own_columns * diag_inv.shape[1],
        pattern,
        panel_l,
        diag_inv,
        smem=1,
    )
    factor_other = permute(factor, mesh, 0, 0, swap=True)
    third = permute(first, mesh, 1, 2)
    near_x = permute(near_z, mesh, None, 1)
    far_x = permute(far_z, mesh, None, 1)
    gathered, partial = call(
        half_kernel,
        [shape(half_rows, sigma_top.shape[1]), shape(half_rows, own_columns)],
        2 * half_rows * half_rows * own_columns,
        sigma_top,
        first,
        second,
        third,
        factor,
        factor_other,
    )
    beside = permute(gathered, mesh, None, 0, swap=True)
    sigma, cross = call(
        panel_kernel,
        [shape(half_rows, own_columns), shape(*diag_inv.shape)],
        2 * half_rows * half_rows * own_columns,
        near_z,
        near_x,
        far_z,
        far_x,
        beside,
        partial,
        factor,
        factor_other,
        scratch=[pltpu.VMEM((half_rows, half_rows), f32)],
    )
    cross_other = permute(cross, mesh, 0, 0, swap=True)
    return sigma, own_part - (cross + cross_other)


def local_any(sigma_top, panel_l, diag_inv, pattern):
    half_rows = panel_l.shape[0]
    local_sn, width = diag_inv.shape[:2]
    row_mask = jnp.repeat(pattern.astype(jnp.float32), W // BLOCK_ROWS, axis=1)
    row_mask = lax.dynamic_slice_in_dim(row_mask, lax.axis_index("pcol") * half_rows, half_rows, 1)
    masked = panel_l.reshape(half_rows, local_sn, width) * jnp.transpose(row_mask)[:, :, None]
    factor = jnp.einsum("wns,nst->wnt", masked, diag_inv, precision=lax.Precision.HIGHEST)
    factor_flat = factor.reshape(half_rows, local_sn * width)
    whole = lax.all_gather(factor_flat, "pcol", axis=0, tiled=True)
    gathered = lax.all_gather(sigma_top, "prow", axis=0, tiled=True)
    sigma = -jnp.einsum("wv,wt->vt", gathered, whole, precision=lax.Precision.HIGHEST)
    sigma_three = sigma.reshape(half_rows, local_sn, width)
    cross = lax.psum(jnp.einsum("wnr,wnt->nrt", factor, sigma_three, precision=lax.Precision.HIGHEST), "pcol")
    own_part = jnp.einsum("nsr,nst->nrt", diag_inv, diag_inv, precision=lax.Precision.HIGHEST)
    return sigma, own_part - cross


def solution(mesh):
    in_specs = (
        P(("cfg", "prow"), "pcol"),
        P(("cfg", "pcol"), "prow"),
        P(("cfg", "prow"), None, None),
        P(("cfg", "prow"), None),
    )
    out_specs = (P(("cfg", "pcol"), "prow"), P(("cfg", "prow"), None, None))
    local = functools.partial(local_eight, mesh) if mesh.shape["prow"] == 8 else local_any
    return jax.shard_map(local, mesh=mesh, in_specs=in_specs, out_specs=out_specs, check_vma=False)
```

```python
import functools

import jax
import jax.numpy as jnp
from jax import lax
from jax.experimental import pallas as pl
from jax.experimental.pallas import tpu as pltpu
from jax.sharding import PartitionSpec as P

W = 1024
BLOCK_ROWS = 8
AXES = ("cfg", "prow", "pcol")
VMEM = pl.BlockSpec(memory_space=pltpu.VMEM)
SMEM = pl.BlockSpec(memory_space=pltpu.SMEM)


def split(value):
    high = value.astype(jnp.bfloat16)
    low = (value - high.astype(jnp.float32)).astype(jnp.bfloat16)
    return high, low


def product(left, right, dims):
    dot = functools.partial(lax.dot_general, dimension_numbers=(dims, ((), ())), preferred_element_type=jnp.float32)
    return dot(left[0], right[0]) + (dot(left[0], right[1]) + dot(left[1], right[0]))


PLAIN = ((1,), (0,))
FIRST = ((0,), (0,))


def factor_kernel(pattern, panel, diag_inv, factor, own_part):
    core = lax.axis_index("pcol")
    rows, width = panel.shape[0], diag_inv.shape[1]
    block = W // BLOCK_ROWS
    for j in range(diag_inv.shape[0]):
        columns = pl.ds(j * width, width)
        inverse = split(diag_inv[j])
        masked = jnp.concatenate(
            [
                panel[pl.ds(r * block, block), columns]
                * pattern[j, core * (rows // block) + r].astype(jnp.float32)
                for r in range(rows // block)
            ],
            axis=0,
        )
        factor[:, columns] = product(split(masked), inverse, PLAIN)
        own_part[j] = product(inverse, inverse, FIRST)


def own_place():
    prow = lax.axis_index("prow")
    return lax.rem(prow, 4), lax.div(prow, 4) == lax.axis_index("pcol")


def places(place):
    beside = place + 1 - 2 * lax.rem(place, 2)
    return beside, lax.rem(place + 2, 4), lax.rem(beside + 2, 4)


def at(place, block):
    return pl.ds(pl.multiple_of(place * block, block), block)


def pieces_kernel(own, first, second):
    place, diagonal = own_place()
    block = own.shape[0]
    half = block // 2

    @pl.when(diagonal)
    def _():
        opposite = at(lax.rem(place + 2, 4), block)
        for piece in (first, second):
            piece[pl.ds(0, block), :] = own[:, at(place, block)]
            piece[pl.ds(block, block), :] = own[:, at(lax.rem(place + 1, 4), block)]

        @pl.when(place < 2)
        def _():
            for piece in (first, second):
                piece[pl.ds(2 * block, half), :] = own[pl.ds(0, half), opposite]

        @pl.when(place >= 2)
        def _():
            turned = own[:, opposite].T
            for piece in (first, second):
                piece[pl.ds(2 * block, half), :] = turned[half:]

    @pl.when(jnp.logical_not(diagonal))
    def _():
        for n, piece in enumerate((first, second)):
            for b in range(2):
                piece[pl.ds(b * block, block), :] = own[:, pl.ds((2 * n + b) * block, block)]
            piece[pl.ds(2 * block, half), :] = jnp.zeros((half, block), jnp.float32)


def symmetric(quadrant, pieces):
    block = quadrant.shape[0] // 4
    half = block // 2
    for piece, place in pieces:
        rows = at(place, block)
        quadrant[rows, at(place, block)] = piece[pl.ds(0, block), :]
        quadrant[rows, at(lax.rem(place + 1, 4), block)] = piece[pl.ds(block, block), :]
        low = lax.rem(place, 2)
        quadrant[
            pl.ds(pl.multiple_of(low * block + lax.div(place, 2) * half, half), half), at(low + 2, block)
        ] = piece[pl.ds(2 * block, half), :]
    for row, column in ((0, 1), (1, 2), (2, 3), (3, 0), (0, 2), (1, 3)):
        rows, columns = pl.ds(row * block, block), pl.ds(column * block, block)
        quadrant[columns, rows] = quadrant[rows, columns].T


def quadrant_kernel(mine_a, mine_b, got1, got2, got3, got4, got5, got6, got7, quadrant):
    place, diagonal = own_place()
    beside, over, across = places(place)
    block = quadrant.shape[0] // 4

    @pl.when(diagonal)
    def _():
        symmetric(quadrant, ((got1, place), (got2, over), (got5, beside), (got7, across)))

    @pl.when(jnp.logical_not(diagonal))
    def _():
        for where, halves in (
            (place, (mine_a, mine_b)),
            (beside, (got1, got4)),
            (over, (got2, got3)),
            (across, (got5, got6)),
        ):
            for n, piece in enumerate(halves):
                for b in range(2):
                    quadrant[at(where, block), pl.ds((2 * n + b) * block, block)] = piece[pl.ds(b * block, block), :]


def near_kernel(mine, got3, got4, got6, quadrant, factor, factor_other, partial, own_quadrant):
    place, diagonal = own_place()
    beside, over, across = places(place)

    @pl.when(diagonal)
    def _():
        symmetric(own_quadrant, ((mine, place), (got3, beside), (got4, over), (got6, across)))
        partial[...] = product(split(own_quadrant[...]), split(factor[...]), PLAIN)

    @pl.when(jnp.logical_not(diagonal))
    def _():
        partial[...] = product(split(quadrant[...]), split(factor_other[...]), FIRST)


def panel_kernel(quadrant, partial, factor, factor_other, sigma, cross):
    _, diagonal = own_place()
    own_factor = split(factor[...])

    @pl.when(diagonal)
    def _():
        sigma[...] = -(partial[...] + product(split(quadrant[...]), split(factor_other[...]), PLAIN))

    @pl.when(jnp.logical_not(diagonal))
    def _():
        sigma[...] = -(partial[...] + product(split(quadrant[...]), own_factor, PLAIN))

    width = cross.shape[1]
    sigma_split = split(sigma[...])
    for j in range(cross.shape[0]):
        columns = slice(j * width, (j + 1) * width)
        cross[j] = product(
            tuple(part[:, columns] for part in own_factor), tuple(part[:, columns] for part in sigma_split), FIRST
        )


def call(kernel, out_shapes, flops, *args, smem=0, scratch=()):
    moved = sum(a.size * 4 for a in args) + sum(4 * o.size for o in out_shapes)
    return pl.pallas_call(
        kernel,
        out_shape=out_shapes,
        in_specs=[SMEM] * smem + [VMEM] * (len(args) - smem),
        out_specs=[VMEM] * len(out_shapes),
        scratch_shapes=scratch,
        cost_estimate=pl.CostEstimate(flops=flops, bytes_accessed=moved, transcendentals=0),
        compiler_params=pltpu.CompilerParams(vmem_limit_bytes=32 * 1024 * 1024),
    )(*args)


def permute(value, mesh, diagonal_step, other_step=None):
    cfgs, prows, cores = (mesh.shape[axis] for axis in AXES)
    pairs = []
    for c in range(cfgs):
        for p in range(prows):
            for k in range(cores):
                to = p ^ (diagonal_step if p // 4 == k else other_step)
                pairs.append(((c * prows + p) * cores + k, (c * prows + to) * cores + (k ^ (p // 4) ^ (to // 4))))
    return lax.ppermute(value, AXES, pairs)


def exchange(value, mesh):
    cfgs, prows, cores = (mesh.shape[axis] for axis in AXES)
    return lax.ppermute(value, AXES, [(d, d ^ 1) for d in range(cfgs * prows * cores)])


def local_eight(mesh, sigma_top, panel_l, diag_inv, pattern):
    f32 = jnp.float32
    half_rows, own_columns = panel_l.shape
    block = sigma_top.shape[0]
    shape = lambda *dims: jax.ShapeDtypeStruct(dims, f32)
    piece = shape(2 * block + block // 2, block)
    mine_a, mine_b = call(pieces_kernel, [piece, piece], 1, sigma_top)
    got1 = permute(mine_a, mesh, 4, 1)
    got2 = permute(mine_a, mesh, 6, 2)
    got3 = permute(mine_b, mesh, 1, 2)
    got4 = permute(mine_b, mesh, 2, 1)
    got5 = permute(got1, mesh, 1, 2)
    got6 = permute(got4, mesh, 1, 2)
    got7 = permute(got2, mesh, 1, 1)

    factor, own_part = call(
        factor_kernel,
        [shape(half_rows, own_columns), shape(*diag_inv.shape)],
        2 * half_rows * own_columns * diag_inv.shape[1],
        pattern,
        panel_l,
        diag_inv,
        smem=1,
    )
    factor_other = exchange(factor, mesh)
    (quadrant,) = call(
        quadrant_kernel,
        [shape(half_rows, half_rows)],
        1,
        mine_a, mine_b, got1, got2, got3, got4, got5, got6, got7,
    )
    quadrant_other = exchange(quadrant, mesh)
    (partial,) = call(
        near_kernel,
        [shape(half_rows, own_columns)],
        2 * half_rows * half_rows * own_columns,
        mine_a, got3, got4, got6, quadrant, factor, factor_other,
        scratch=[pltpu.VMEM((half_rows, half_rows), f32)],
    )
    sigma, cross = call(
        panel_kernel,
        [shape(half_rows, own_columns), shape(*diag_inv.shape)],
        2 * half_rows * half_rows * own_columns,
        quadrant_other, partial, factor, factor_other,
    )
    cross_other = exchange(cross, mesh)
    return sigma, own_part - (cross + cross_other)


def local_any(sigma_top, panel_l, diag_inv, pattern):
    half_rows = panel_l.shape[0]
    local_sn, width = diag_inv.shape[:2]
    row_mask = jnp.repeat(pattern.astype(jnp.float32), W // BLOCK_ROWS, axis=1)
    row_mask = lax.dynamic_slice_in_dim(row_mask, lax.axis_index("pcol") * half_rows, half_rows, 1)
    masked = panel_l.reshape(half_rows, local_sn, width) * jnp.transpose(row_mask)[:, :, None]
    factor = jnp.einsum("wns,nst->wnt", masked, diag_inv, precision=lax.Precision.HIGHEST)
    factor_flat = factor.reshape(half_rows, local_sn * width)
    whole = lax.all_gather(factor_flat, "pcol", axis=0, tiled=True)
    gathered = lax.all_gather(sigma_top, "prow", axis=0, tiled=True)
    sigma = -jnp.einsum("wv,wt->vt", gathered, whole, precision=lax.Precision.HIGHEST)
    sigma_three = sigma.reshape(half_rows, local_sn, width)
    cross = lax.psum(jnp.einsum("wnr,wnt->nrt", factor, sigma_three, precision=lax.Precision.HIGHEST), "pcol")
    own_part = jnp.einsum("nsr,nst->nrt", diag_inv, diag_inv, precision=lax.Precision.HIGHEST)
    return sigma, own_part - cross


def solution(mesh):
    in_specs = (
        P(("cfg", "prow"), "pcol"),
        P(("cfg", "pcol"), "prow"),
        P(("cfg", "prow"), None, None),
        P(("cfg", "prow"), None),
    )
    out_specs = (P(("cfg", "pcol"), "prow"), P(("cfg", "prow"), None, None))
    local = functools.partial(local_eight, mesh) if mesh.shape["prow"] == 8 else local_any
    return jax.shard_map(local, mesh=mesh, in_specs=in_specs, out_specs=out_specs, check_vma=False)
```

```python
import functools

import jax
import jax.numpy as jnp
from jax import lax
from jax.experimental import pallas as pl
from jax.experimental.pallas import tpu as pltpu
from jax.sharding import PartitionSpec as P

W = 1024
BLOCK_ROWS = 8
AXES = ("cfg", "prow", "pcol")
VMEM = pl.BlockSpec(memory_space=pltpu.VMEM)
SMEM = pl.BlockSpec(memory_space=pltpu.SMEM)


def split(value):
    high = value.astype(jnp.bfloat16)
    low = (value - high.astype(jnp.float32)).astype(jnp.bfloat16)
    return high, low


def product(left, right, dims):
    dot = functools.partial(lax.dot_general, dimension_numbers=(dims, ((), ())), preferred_element_type=jnp.float32)
    return dot(left[0], right[0]) + (dot(left[0], right[1]) + dot(left[1], right[0]))


PLAIN = ((1,), (0,))
FIRST = ((0,), (0,))


def factor_kernel(mask, panel, diag_inv, factor):
    children, width = diag_inv.shape[:2]
    here = mask.shape[0] // children
    block = panel.shape[0] // here
    for j in range(children):
        columns = pl.ds(j * width, width)
        masked = jnp.concatenate(
            [panel[pl.ds(r * block, block), columns] * mask[pl.ds(j * here + r, 1), :] for r in range(here)], axis=0
        )
        factor[:, columns] = product(split(masked), split(diag_inv[j]), PLAIN)


def own_place():
    prow = lax.axis_index("prow")
    return lax.rem(prow, 4), lax.div(prow, 4) == lax.axis_index("pcol")


def places(place):
    beside = place + 1 - 2 * lax.rem(place, 2)
    return beside, lax.rem(place + 2, 4), lax.rem(beside + 2, 4)


def at(place, block):
    return pl.ds(pl.multiple_of(place * block, block), block)


def pieces_kernel(
    sigma_top, pattern, panel, diag_inv, first, second, mask, panel_here, inverse_here, own, pattern_here, sems
):
    place, diagonal = own_place()
    loads = [
        pltpu.make_async_copy(source, here, sems.at[n])
        for n, (source, here) in enumerate(
            ((sigma_top, own), (pattern, pattern_here), (panel, panel_here), (diag_inv, inverse_here))
        )
    ]
    for load in loads:
        load.start()
    loads[0].wait()
    block = own.shape[0]
    half = block // 2

    @pl.when(diagonal)
    def _():
        opposite = at(lax.rem(place + 2, 4), block)
        for piece in (first, second):
            piece[pl.ds(0, block), :] = own[:, at(place, block)]
            piece[pl.ds(block, block), :] = own[:, at(lax.rem(place + 1, 4), block)]

        @pl.when(place < 2)
        def _():
            for piece in (first, second):
                piece[pl.ds(2 * block, half), :] = own[pl.ds(0, half), opposite]

        @pl.when(place >= 2)
        def _():
            turned = own[:, opposite].T
            for piece in (first, second):
                piece[pl.ds(2 * block, half), :] = turned[half:]

    @pl.when(jnp.logical_not(diagonal))
    def _():
        for n, piece in enumerate((first, second)):
            for b in range(2):
                piece[pl.ds(b * block, block), :] = own[:, pl.ds((2 * n + b) * block, block)]
            piece[pl.ds(2 * block, half), :] = jnp.zeros((half, block), jnp.float32)

    loads[1].wait()
    core = lax.axis_index("pcol")
    here = mask.shape[0] // pattern.shape[0]
    for j in range(pattern.shape[0]):
        for r in range(here):
            kept = pattern_here[j, core * here + r].astype(jnp.float32)
            mask[pl.ds(j * here + r, 1), :] = jnp.full((1, mask.shape[1]), kept, jnp.float32)
    loads[2].wait()
    loads[3].wait()


def parts(piece):
    block = piece.shape[1]
    return [piece.at[pl.ds(n * block, min(block, piece.shape[0] - n * block))] for n in range(3)]


def symmetric(quadrant, pieces):
    block = quadrant.shape[0] // 4
    half = block // 2
    for piece, place in pieces:
        rows = at(place, block)
        here, following, opposite = piece
        quadrant[rows, at(place, block)] = here[...]
        quadrant[rows, at(lax.rem(place + 1, 4), block)] = following[...]
        low = lax.rem(place, 2)
        quadrant[
            pl.ds(pl.multiple_of(low * block + lax.div(place, 2) * half, half), half), at(low + 2, block)
        ] = opposite[...]
    for row, column in ((0, 1), (1, 2), (2, 3), (3, 0), (0, 2), (1, 3)):
        rows, columns = pl.ds(row * block, block), pl.ds(column * block, block)
        quadrant[columns, rows] = quadrant[rows, columns].T


def row_blocks(quadrant, where, halves):
    block = quadrant.shape[0] // 4
    for n, piece in enumerate(halves):
        for b in range(2):
            quadrant[at(where, block), pl.ds((2 * n + b) * block, block)] = piece[pl.ds(b * block, block), :]


def own_half_kernel(mine_a, mine_b, got1, got2, got3, got4, got5, got6, quadrant, sent_a, sent_b):
    place, diagonal = own_place()
    beside, over, across = places(place)
    rows, block = sent_a.shape[0], quadrant.shape[0] // 4

    @pl.when(diagonal)
    def _():
        symmetric(
            quadrant,
            ((parts(mine_a), place), (parts(got3), beside), (parts(got4), over), (parts(got6), across)),
        )
        for n, piece in enumerate((got1, got5, got2)):
            rest = piece.shape[0] - rows
            sent_a[:, pl.ds(n * block, block)] = piece[pl.ds(0, rows), :]
            sent_a[pl.ds(n * rest, rest), pl.ds(3 * block, block)] = piece[pl.ds(rows, rest), :]

    @pl.when(jnp.logical_not(diagonal))
    def _():
        row_blocks(quadrant, place, (mine_a, mine_b))
        row_blocks(quadrant, beside, (got1, got4))
        row_blocks(quadrant, over, (got2, got3))
        row_blocks(quadrant, across, (got5, got6))
        sent_a[...] = quadrant[pl.ds(0, rows), :]
        sent_b[...] = quadrant[pl.ds(rows, rows), :]


def columns_of(value, j, width):
    return tuple(part[:, j * width : (j + 1) * width] for part in value)


def near_kernel(
    quadrant, factor, factor_other, diag_inv, partial, cross, base, far_high, far_low, turned_high, turned_low
):
    _, diagonal = own_place()
    width = cross.shape[1]

    def half(near, far):
        far_high[...], far_low[...] = split(far[...])
        turned_high[...], turned_low[...] = split(far[...].T)
        partial[...] = product(split(quadrant[...]), split(near[...]), FIRST)

    @pl.when(diagonal)
    def _():
        half(factor, factor_other)
        own, value = split(factor[...]), split(partial[...])
        for j in range(cross.shape[0]):
            cross[j] = product(columns_of(own, j, width), columns_of(value, j, width), FIRST)

    @pl.when(jnp.logical_not(diagonal))
    def _():
        half(factor_other, factor)
        value = split(partial[...])
        for j in range(cross.shape[0]):
            rows = pl.ds(j * width, width)
            mixed = product((turned_high[rows, :], turned_low[rows, :]), columns_of(value, j, width), PLAIN)
            cross[j] = mixed + mixed.T

    for j in range(cross.shape[0]):
        inverse = split(diag_inv[j])
        base[j] = cross[j] + product(inverse, inverse, FIRST)


def far_kernel(got1, got2, got5, got7, far_high, far_low, turned_high, turned_low, cross, quadrant):
    place, diagonal = own_place()
    beside, over, across = places(place)
    width = cross.shape[1]

    @pl.when(diagonal)
    def _():
        symmetric(
            quadrant,
            ((parts(got1), place), (parts(got2), over), (parts(got5), beside), (parts(got7), across)),
        )
        value = split(product(split(quadrant[...]), (far_high[...], far_low[...]), PLAIN))
        for j in range(cross.shape[0]):
            rows = pl.ds(j * width, width)
            cross[j] = product((turned_high[rows, :], turned_low[rows, :]), columns_of(value, j, width), PLAIN)


def panel_kernel(
    early_a, early_b, late, partial, far_high, far_low, turned_high, turned_low, base, near_other, far,
    sigma, diag, quadrant, sigma_here, diag_here, sigma_sems, diag_sems,
):
    place, diagonal = own_place()
    beside, over, across = places(place)
    width = diag.shape[1]
    children = range(diag.shape[0])
    chunk = sigma.shape[0] // sigma_sems.shape[0]
    chunks = [pl.ds(c * chunk, chunk) for c in range(sigma_sems.shape[0])]
    sigma_stores = [
        pltpu.make_async_copy(sigma_here.at[rows], sigma.at[rows], sigma_sems.at[c]) for c, rows in enumerate(chunks)
    ]
    diag_stores = [pltpu.make_async_copy(diag_here.at[j], diag.at[j], diag_sems.at[j]) for j in children]

    @pl.when(diagonal)
    def _():
        for j in children:
            diag_here[j] = base[j] + (near_other[j] + far[j])
            diag_stores[j].start()
        far_rows = far_high[...], far_low[...]
        early = [ref[pl.ds(c * chunk, chunk), :] for ref in (early_a, early_b) for c in range(ref.shape[0] // chunk)]
        for rows, store, here in zip(chunks, sigma_stores, early):
            sigma_here[rows, :] = -(partial[rows, :] + product(split(here), far_rows, PLAIN))
            store.start()

    @pl.when(jnp.logical_not(diagonal))
    def _():
        block = late.shape[1]
        half = block // 2
        pieces = [
            [early_a.at[pl.ds(m * block, block), pl.ds(n * block, block)] for m in range(2)]
            + [early_a.at[pl.ds(n * half, half), pl.ds(3 * block, block)]]
            for n in range(3)
        ]
        symmetric(
            quadrant, ((pieces[0], place), (pieces[1], beside), (pieces[2], over), (parts(late), across))
        )
        far_rows = far_high[...], far_low[...]
        values = []
        for rows, store in zip(chunks, sigma_stores):
            last = product(split(quadrant[rows, :]), far_rows, PLAIN)
            sigma_here[rows, :] = -(partial[rows, :] + last)
            store.start()
            values.append(split(last))
        value = tuple(jnp.concatenate(parts, axis=0) for parts in zip(*values))
        for j in children:
            turned = pl.ds(j * width, width)
            inner = product((turned_high[turned, :], turned_low[turned, :]), columns_of(value, j, width), PLAIN)
            diag_here[j] = (base[j] + near_other[j]) + inner
            diag_stores[j].start()

    for store in (*sigma_stores, *diag_stores):
        store.wait()


def call(kernel, out_shapes, flops, *args, specs=None, out_specs=None, scratch=()):
    moved = sum(a.size * a.dtype.itemsize for a in (*args, *out_shapes))
    return pl.pallas_call(
        kernel,
        out_shape=out_shapes,
        in_specs=specs or [VMEM] * len(args),
        out_specs=out_specs or [VMEM] * len(out_shapes),
        scratch_shapes=scratch,
        cost_estimate=pl.CostEstimate(flops=flops, bytes_accessed=moved, transcendentals=0),
        compiler_params=pltpu.CompilerParams(vmem_limit_bytes=32 * 1024 * 1024),
    )(*args)


def permute(value, mesh, diagonal_step, other_step=None):
    cfgs, prows, cores = (mesh.shape[axis] for axis in AXES)
    pairs = []
    for c in range(cfgs):
        for p in range(prows):
            for k in range(cores):
                to = p ^ (diagonal_step if p // 4 == k else other_step)
                pairs.append(((c * prows + p) * cores + k, (c * prows + to) * cores + (k ^ (p // 4) ^ (to // 4))))
    return lax.ppermute(value, AXES, pairs)


def exchange(value, mesh):
    cfgs, prows, cores = (mesh.shape[axis] for axis in AXES)
    return lax.ppermute(value, AXES, [(d, d ^ 1) for d in range(cfgs * prows * cores)])


def local_eight(mesh, sigma_top, panel_l, diag_inv, pattern):
    f32 = jnp.float32
    half_rows, own_columns = panel_l.shape
    block = sigma_top.shape[0]
    local_sn, width = diag_inv.shape[:2]
    shape = lambda *dims: jax.ShapeDtypeStruct(dims, f32)
    size = 2 * block + block // 2
    panel, square = shape(half_rows, own_columns), shape(half_rows, half_rows)
    children = shape(*diag_inv.shape)
    halves = [jax.ShapeDtypeStruct((half_rows, own_columns), jnp.bfloat16)] * 2
    turned = [jax.ShapeDtypeStruct((own_columns, half_rows), jnp.bfloat16)] * 2
    anywhere = pl.BlockSpec(memory_space=pl.ANY)
    in_hbm = lambda value: pltpu.with_memory_space_constraint(value, pltpu.HBM)
    step = 2 * half_rows * half_rows * own_columns
    mine_a, mine_b, mask, panel_here, inverse_here = call(
        pieces_kernel,
        [shape(size, block)] * 2 + [shape(local_sn * (half_rows // block), width), panel, children],
        1,
        in_hbm(sigma_top),
        in_hbm(pattern),
        in_hbm(panel_l),
        in_hbm(diag_inv),
        specs=[anywhere] * 4,
        scratch=[
            pltpu.VMEM(sigma_top.shape, f32),
            pltpu.SMEM(pattern.shape, jnp.int32),
            pltpu.SemaphoreType.DMA((4,)),
        ],
    )
    got1 = permute(mine_a, mesh, 4, 1)
    got2 = permute(mine_a, mesh, 6, 2)
    got3 = permute(mine_b, mesh, 1, 2)
    got4 = permute(mine_b, mesh, 2, 1)
    got5 = permute(got1, mesh, 1, 2)
    got6 = permute(got4, mesh, 1, 2)
    got7 = permute(got2, mesh, 1, 1)
    (factor,) = call(
        factor_kernel,
        [panel],
        1,
        mask,
        panel_here,
        inverse_here,
    )
    factor_other = exchange(factor, mesh)
    own_half, sent_a, sent_b = call(
        own_half_kernel,
        [square, shape(half_rows // 2, half_rows), shape(half_rows // 2, half_rows)],
        36 * step,
        mine_a, mine_b, got1, got2, got3, got4, got5, got6,
    )
    early_a, early_b = exchange(sent_a, mesh), exchange(sent_b, mesh)
    partial, near, base, *far_rows = call(
        near_kernel, [panel, children, children, *halves, *turned], 1, own_half, factor, factor_other, inverse_here
    )
    near_other = exchange(near, mesh)
    late = exchange(got7, mesh)
    (far,) = call(
        far_kernel,
        [children],
        16 * step,
        got1, got2, got5, got7, *far_rows,
        scratch=[pltpu.VMEM(square.shape, f32)],
    )
    return tuple(
        call(
            panel_kernel,
            [panel, children],
            1,
            early_a, early_b, late, partial, *far_rows, base, near_other, far,
            out_specs=[anywhere] * 2,
            scratch=[
                pltpu.VMEM(square.shape, f32),
                pltpu.VMEM(panel.shape, f32),
                pltpu.VMEM(children.shape, f32),
                pltpu.SemaphoreType.DMA((half_rows // block,)),
                pltpu.SemaphoreType.DMA((local_sn,)),
            ],
        )
    )


def local_any(sigma_top, panel_l, diag_inv, pattern):
    half_rows = panel_l.shape[0]
    local_sn, width = diag_inv.shape[:2]
    row_mask = jnp.repeat(pattern.astype(jnp.float32), W // BLOCK_ROWS, axis=1)
    row_mask = lax.dynamic_slice_in_dim(row_mask, lax.axis_index("pcol") * half_rows, half_rows, 1)
    masked = panel_l.reshape(half_rows, local_sn, width) * jnp.transpose(row_mask)[:, :, None]
    factor = jnp.einsum("wns,nst->wnt", masked, diag_inv, precision=lax.Precision.HIGHEST)
    factor_flat = factor.reshape(half_rows, local_sn * width)
    whole = lax.all_gather(factor_flat, "pcol", axis=0, tiled=True)
    gathered = lax.all_gather(sigma_top, "prow", axis=0, tiled=True)
    sigma = -jnp.einsum("wv,wt->vt", gathered, whole, precision=lax.Precision.HIGHEST)
    sigma_three = sigma.reshape(half_rows, local_sn, width)
    cross = lax.psum(jnp.einsum("wnr,wnt->nrt", factor, sigma_three, precision=lax.Precision.HIGHEST), "pcol")
    own_part = jnp.einsum("nsr,nst->nrt", diag_inv, diag_inv, precision=lax.Precision.HIGHEST)
    return sigma, own_part - cross


def solution(mesh):
    in_specs = (
        P(("cfg", "prow"), "pcol"),
        P(("cfg", "pcol"), "prow"),
        P(("cfg", "prow"), None, None),
        P(("cfg", "prow"), None),
    )
    out_specs = (P(("cfg", "pcol"), "prow"), P(("cfg", "prow"), None, None))
    local = functools.partial(local_eight, mesh) if mesh.shape["prow"] == 8 else local_any
    return jax.shard_map(local, mesh=mesh, in_specs=in_specs, out_specs=out_specs, check_vma=False)
```

```python
import functools

import jax
import jax.numpy as jnp
from jax import lax
from jax.experimental import pallas as pl
from jax.experimental.pallas import tpu as pltpu
from jax.sharding import PartitionSpec as P

W = 1024
BLOCK_ROWS = 8
SPARE = 8
AXES = ("cfg", "prow", "pcol")
VMEM = pl.BlockSpec(memory_space=pltpu.VMEM)
SMEM = pl.BlockSpec(memory_space=pltpu.SMEM)


def split(value):
    high = value.astype(jnp.bfloat16)
    low = (value - high.astype(jnp.float32)).astype(jnp.bfloat16)
    return high, low


def product(left, right, dims):
    dot = functools.partial(lax.dot_general, dimension_numbers=(dims, ((), ())), preferred_element_type=jnp.float32)
    return dot(left[0], right[0]) + (dot(left[0], right[1]) + dot(left[1], right[0]))


PLAIN = ((1,), (0,))
FIRST = ((0,), (0,))


def factor_kernel(mask, panel, diag_inv, factor):
    children, width = diag_inv.shape[:2]
    here = mask.shape[0] // children
    block = panel.shape[0] // here
    for j in range(children):
        columns = pl.ds(j * width, width)
        masked = jnp.concatenate(
            [panel[pl.ds(r * block, block), columns] * mask[pl.ds(j * here + r, 1), :] for r in range(here)], axis=0
        )
        factor[:, columns] = product(split(masked), split(diag_inv[j]), PLAIN)


def own_place():
    prow = lax.axis_index("prow")
    return lax.rem(prow, 4), lax.div(prow, 4) == lax.axis_index("pcol")


def places(place):
    beside = place + 1 - 2 * lax.rem(place, 2)
    return beside, lax.rem(place + 2, 4), lax.rem(beside + 2, 4)


def at(place, block):
    return pl.ds(pl.multiple_of(place * block, block), block)


def parts(piece):
    block = piece.shape[1]
    half, last = block // 2, 2 * block
    return [piece.at[pl.ds(start, size)] for start, size in ((0, block), (block, half), (block + half, half), (last, SPARE))]


def folded(block):
    half = block.shape[0] // 2
    top, bottom = block[:half], block[half:]
    row, lane = (lax.broadcasted_iota(jnp.int32, top.shape, axis) for axis in (0, 1))
    top = jnp.where((lane < half) & (row > lane), pltpu.roll(bottom, half, 1), top)
    return top, jnp.sum(jnp.where(row == lane - half, bottom, 0.0), axis=0, keepdims=True)


def unfolded(top, ends):
    half = top.shape[0]
    row, lane = (lax.broadcasted_iota(jnp.int32, top.shape, axis) for axis in (0, 1))
    turned = jnp.concatenate([top, jnp.zeros_like(top)], axis=0).T
    upper = jnp.where((lane < half) & (row > lane), turned[:half], top)
    own = jnp.where(row < lane - half, pltpu.roll(turned[:half], half, 1), ends)
    own = jnp.where(row > lane - half, pltpu.roll(top, half, 1), own)
    return jnp.concatenate([upper, jnp.where(lane < half, turned[half:], own)], axis=0)


def pieces_kernel(
    sigma_top, pattern, panel, diag_inv, first, second, mask, panel_here, inverse_here, own, pattern_here, sems
):
    place, diagonal = own_place()
    loads = [
        pltpu.make_async_copy(source, here, sems.at[n])
        for n, (source, here) in enumerate(
            ((sigma_top, own), (pattern, pattern_here), (panel, panel_here), (diag_inv, inverse_here))
        )
    ]
    for load in loads:
        load.start()
    loads[0].wait()
    block = own.shape[0]
    half = block // 2

    @pl.when(diagonal)
    def _():
        opposite = at(lax.rem(place + 2, 4), block)
        top, ends = folded(own[:, at(place, block)])
        for piece in (first, second):
            following, _, folded_top, folded_ends = parts(piece)
            following[...] = own[:, at(lax.rem(place + 1, 4), block)]
            folded_top[...] = top
            folded_ends[...] = jnp.broadcast_to(ends, folded_ends.shape)

        @pl.when(place < 2)
        def _():
            for piece in (first, second):
                parts(piece)[1][...] = own[pl.ds(0, half), opposite]

        @pl.when(place >= 2)
        def _():
            turned = own[:, opposite].T
            for piece in (first, second):
                parts(piece)[1][...] = turned[half:]

    @pl.when(jnp.logical_not(diagonal))
    def _():
        for n, piece in enumerate((first, second)):
            for b in range(2):
                piece[pl.ds(b * block, block), :] = own[:, pl.ds((2 * n + b) * block, block)]
            piece[pl.ds(2 * block, SPARE), :] = jnp.zeros((SPARE, block), jnp.float32)

    loads[1].wait()
    core = lax.axis_index("pcol")
    here = mask.shape[0] // pattern.shape[0]
    for j in range(pattern.shape[0]):
        for r in range(here):
            kept = pattern_here[j, core * here + r].astype(jnp.float32)
            mask[pl.ds(j * here + r, 1), :] = jnp.full((1, mask.shape[1]), kept, jnp.float32)
    loads[2].wait()
    loads[3].wait()


def symmetric(quadrant, pieces):
    block = quadrant.shape[0] // 4
    half = block // 2
    for piece, place in pieces:
        rows = at(place, block)
        following, opposite, top, ends = piece
        quadrant[rows, at(place, block)] = unfolded(top[...], ends[pl.ds(0, 1), :])
        quadrant[rows, at(lax.rem(place + 1, 4), block)] = following[...]
        low = lax.rem(place, 2)
        quadrant[
            pl.ds(pl.multiple_of(low * block + lax.div(place, 2) * half, half), half), at(low + 2, block)
        ] = opposite[...]
    for row, column in ((0, 1), (1, 2), (2, 3), (3, 0), (0, 2), (1, 3)):
        rows, columns = pl.ds(row * block, block), pl.ds(column * block, block)
        quadrant[columns, rows] = quadrant[rows, columns].T


def row_blocks(quadrant, where, halves):
    block = quadrant.shape[0] // 4
    for n, piece in enumerate(halves):
        for b in range(2):
            quadrant[at(where, block), pl.ds((2 * n + b) * block, block)] = piece[pl.ds(b * block, block), :]


def own_half_kernel(mine_a, mine_b, got1, got2, got3, got4, got5, got6, quadrant, sent_a, sent_b):
    place, diagonal = own_place()
    beside, over, across = places(place)
    rows, block = sent_a.shape[0], quadrant.shape[0] // 4

    @pl.when(diagonal)
    def _():
        symmetric(
            quadrant,
            ((parts(mine_a), place), (parts(got3), beside), (parts(got4), over), (parts(got6), across)),
        )
        for n, piece in enumerate((got1, got5, got2)):
            rest = piece.shape[0] - rows
            sent_a[:, pl.ds(n * block, block)] = piece[pl.ds(0, rows), :]
            sent_a[pl.ds(n * rest, rest), pl.ds(3 * block, block)] = piece[pl.ds(rows, rest), :]

    @pl.when(jnp.logical_not(diagonal))
    def _():
        row_blocks(quadrant, place, (mine_a, mine_b))
        row_blocks(quadrant, beside, (got1, got4))
        row_blocks(quadrant, over, (got2, got3))
        row_blocks(quadrant, across, (got5, got6))
        sent_a[...] = quadrant[pl.ds(0, rows), :]
        sent_b[...] = quadrant[pl.ds(rows, rows), :]


def columns_of(value, j, width):
    return tuple(part[:, j * width : (j + 1) * width] for part in value)


def split_kernel(factor, factor_other, diag_inv, far_high, far_low, turned_high, turned_low, own_part):
    _, diagonal = own_place()

    def write(rows):
        far_high[...], far_low[...] = split(rows)
        turned_high[...], turned_low[...] = split(rows.T)

    @pl.when(diagonal)
    def _():
        write(factor_other[...])

    @pl.when(jnp.logical_not(diagonal))
    def _():
        write(factor[...])

    for j in range(own_part.shape[0]):
        inverse = split(diag_inv[j])
        own_part[j] = product(inverse, inverse, FIRST)


def near_kernel(quadrant, factor, factor_other, turned_high, turned_low, partial, cross):
    _, diagonal = own_place()
    width = cross.shape[1]

    @pl.when(diagonal)
    def _():
        own = split(factor[...])
        partial[...] = product(split(quadrant[...]), own, PLAIN)
        value = split(partial[...])
        for j in range(cross.shape[0]):
            cross[j] = product(columns_of(own, j, width), columns_of(value, j, width), FIRST)

    @pl.when(jnp.logical_not(diagonal))
    def _():
        partial[...] = product(split(quadrant[...]), split(factor_other[...]), FIRST)
        value = split(partial[...])
        for j in range(cross.shape[0]):
            rows = pl.ds(j * width, width)
            mixed = product((turned_high[rows, :], turned_low[rows, :]), columns_of(value, j, width), PLAIN)
            cross[j] = mixed + mixed.T


def again_kernel(got, same):
    same[...] = got[...]


def far_kernel(got1, got2, got5, got7, far_high, far_low, turned_high, turned_low, cross, quadrant):
    place, diagonal = own_place()
    beside, over, across = places(place)
    width = cross.shape[1]

    @pl.when(diagonal)
    def _():
        symmetric(
            quadrant,
            ((parts(got1), place), (parts(got2), over), (parts(got5), beside), (parts(got7), across)),
        )
        value = split(product(split(quadrant[...]), (far_high[...], far_low[...]), PLAIN))
        for j in range(cross.shape[0]):
            rows = pl.ds(j * width, width)
            cross[j] = product((turned_high[rows, :], turned_low[rows, :]), columns_of(value, j, width), PLAIN)


def panel_kernel(
    early_a, early_b, late, partial, far_high, far_low, turned_high, turned_low, own_part, near, near_other, far,
    sigma, diag, quadrant, sigma_here, diag_here, sigma_sems, diag_sems,
):
    place, diagonal = own_place()
    beside, over, across = places(place)
    width = diag.shape[1]
    children = range(diag.shape[0])
    chunk = sigma.shape[0] // sigma_sems.shape[0]
    chunks = [pl.ds(c * chunk, chunk) for c in range(sigma_sems.shape[0])]
    sigma_stores = [
        pltpu.make_async_copy(sigma_here.at[rows], sigma.at[rows], sigma_sems.at[c]) for c, rows in enumerate(chunks)
    ]
    diag_stores = [pltpu.make_async_copy(diag_here.at[j], diag.at[j], diag_sems.at[j]) for j in children]

    @pl.when(diagonal)
    def _():
        for j in children:
            diag_here[j] = (own_part[j] + near[j]) + (near_other[j] + far[j])
            diag_stores[j].start()
        far_rows = far_high[...], far_low[...]
        early = [ref[pl.ds(c * chunk, chunk), :] for ref in (early_a, early_b) for c in range(ref.shape[0] // chunk)]
        for rows, store, here in zip(chunks, sigma_stores, early):
            sigma_here[rows, :] = -(partial[rows, :] + product(split(here), far_rows, PLAIN))
            store.start()

    @pl.when(jnp.logical_not(diagonal))
    def _():
        block = late.shape[1]
        half = block // 2
        pieces = [
            [
                early_a.at[pl.ds(start, size), pl.ds(n * block, block)]
                for start, size in ((0, block), (block, half), (block + half, half))
            ]
            + [early_a.at[pl.ds(n * SPARE, SPARE), pl.ds(3 * block, block)]]
            for n in range(3)
        ]
        symmetric(
            quadrant, ((pieces[0], place), (pieces[1], beside), (pieces[2], over), (parts(late), across))
        )
        far_rows = far_high[...], far_low[...]
        values = []
        for rows, store in zip(chunks, sigma_stores):
            last = product(split(quadrant[rows, :]), far_rows, PLAIN)
            sigma_here[rows, :] = -(partial[rows, :] + last)
            store.start()
            values.append(split(last))
        value = tuple(jnp.concatenate(parts, axis=0) for parts in zip(*values))
        for j in children:
            turned = pl.ds(j * width, width)
            inner = product((turned_high[turned, :], turned_low[turned, :]), columns_of(value, j, width), PLAIN)
            diag_here[j] = (own_part[j] + near[j]) + (near_other[j] + inner)
            diag_stores[j].start()

    for store in (*sigma_stores, *diag_stores):
        store.wait()


def call(kernel, out_shapes, flops, *args, specs=None, out_specs=None, scratch=()):
    moved = sum(a.size * a.dtype.itemsize for a in (*args, *out_shapes))
    return pl.pallas_call(
        kernel,
        out_shape=out_shapes,
        in_specs=specs or [VMEM] * len(args),
        out_specs=out_specs or [VMEM] * len(out_shapes),
        scratch_shapes=scratch,
        cost_estimate=pl.CostEstimate(flops=flops, bytes_accessed=moved, transcendentals=0),
        compiler_params=pltpu.CompilerParams(vmem_limit_bytes=32 * 1024 * 1024),
    )(*args)


def permute(value, mesh, diagonal_step, other_step=None):
    cfgs, prows, cores = (mesh.shape[axis] for axis in AXES)
    pairs = []
    for c in range(cfgs):
        for p in range(prows):
            for k in range(cores):
                step = diagonal_step if p // 4 == k else other_step
                to_cfg, to = (cfgs - 1 - c, p) if step is None else (c, p ^ step)
                pairs.append(((c * prows + p) * cores + k, (to_cfg * prows + to) * cores + (k ^ (p // 4) ^ (to // 4))))
    return lax.ppermute(value, AXES, pairs)


def exchange(value, mesh):
    cfgs, prows, cores = (mesh.shape[axis] for axis in AXES)
    return lax.ppermute(value, AXES, [(d, d ^ 1) for d in range(cfgs * prows * cores)])


def local_eight(mesh, sigma_top, panel_l, diag_inv, pattern):
    f32 = jnp.float32
    half_rows, own_columns = panel_l.shape
    block = sigma_top.shape[0]
    local_sn, width = diag_inv.shape[:2]
    shape = lambda *dims: jax.ShapeDtypeStruct(dims, f32)
    size = 2 * block + SPARE
    panel, square = shape(half_rows, own_columns), shape(half_rows, half_rows)
    children = shape(*diag_inv.shape)
    halves = [jax.ShapeDtypeStruct((half_rows, own_columns), jnp.bfloat16)] * 2
    turned = [jax.ShapeDtypeStruct((own_columns, half_rows), jnp.bfloat16)] * 2
    anywhere = pl.BlockSpec(memory_space=pl.ANY)
    in_hbm = lambda value: pltpu.with_memory_space_constraint(value, pltpu.HBM)
    step = 2 * half_rows * half_rows * own_columns
    mine_a, mine_b, mask, panel_here, inverse_here = call(
        pieces_kernel,
        [shape(size, block)] * 2 + [shape(local_sn * (half_rows // block), width), panel, children],
        1,
        in_hbm(sigma_top),
        in_hbm(pattern),
        in_hbm(panel_l),
        in_hbm(diag_inv),
        specs=[anywhere] * 4,
        scratch=[
            pltpu.VMEM(sigma_top.shape, f32),
            pltpu.SMEM(pattern.shape, jnp.int32),
            pltpu.SemaphoreType.DMA((4,)),
        ],
    )
    got1 = permute(mine_a, mesh, 4, 1)
    got2 = permute(mine_a, mesh, 6, 2)
    got3 = permute(mine_b, mesh, 1, 2)
    got4 = permute(mine_b, mesh, 2, 1)
    got5 = permute(got1, mesh, 1, 2)
    got6 = permute(got4, mesh, 1, 2)
    (got2_again,) = call(again_kernel, [shape(size, block)], 40 * step, got2)
    got7 = permute(got2_again, mesh, 1)
    (factor,) = call(
        factor_kernel,
        [panel],
        1,
        mask,
        panel_here,
        inverse_here,
    )
    factor_other = exchange(factor, mesh)
    own_half, sent_a, sent_b = call(
        own_half_kernel,
        [square, shape(half_rows // 2, half_rows), shape(half_rows // 2, half_rows)],
        36 * step,
        mine_a, mine_b, got1, got2, got3, got4, got5, got6,
    )
    early_a, early_b = exchange(sent_a, mesh), exchange(sent_b, mesh)
    *far_rows, own_part = call(split_kernel, [*halves, *turned, children], 1, factor, factor_other, inverse_here)
    partial, near = call(near_kernel, [panel, children], 1, own_half, factor, factor_other, *far_rows[2:])
    near_other = exchange(near, mesh)
    late = exchange(got7, mesh)
    (far,) = call(
        far_kernel,
        [children],
        16 * step,
        got1, got2, got5, got7, *far_rows,
        scratch=[pltpu.VMEM(square.shape, f32)],
    )
    return tuple(
        call(
            panel_kernel,
            [panel, children],
            1,
            early_a, early_b, late, partial, *far_rows, own_part, near, near_other, far,
            out_specs=[anywhere] * 2,
            scratch=[
                pltpu.VMEM(square.shape, f32),
                pltpu.VMEM(panel.shape, f32),
                pltpu.VMEM(children.shape, f32),
                pltpu.SemaphoreType.DMA((half_rows // block,)),
                pltpu.SemaphoreType.DMA((local_sn,)),
            ],
        )
    )


def local_any(sigma_top, panel_l, diag_inv, pattern):
    half_rows = panel_l.shape[0]
    local_sn, width = diag_inv.shape[:2]
    row_mask = jnp.repeat(pattern.astype(jnp.float32), W // BLOCK_ROWS, axis=1)
    row_mask = lax.dynamic_slice_in_dim(row_mask, lax.axis_index("pcol") * half_rows, half_rows, 1)
    masked = panel_l.reshape(half_rows, local_sn, width) * jnp.transpose(row_mask)[:, :, None]
    factor = jnp.einsum("wns,nst->wnt", masked, diag_inv, precision=lax.Precision.HIGHEST)
    factor_flat = factor.reshape(half_rows, local_sn * width)
    whole = lax.all_gather(factor_flat, "pcol", axis=0, tiled=True)
    gathered = lax.all_gather(sigma_top, "prow", axis=0, tiled=True)
    sigma = -jnp.einsum("wv,wt->vt", gathered, whole, precision=lax.Precision.HIGHEST)
    sigma_three = sigma.reshape(half_rows, local_sn, width)
    cross = lax.psum(jnp.einsum("wnr,wnt->nrt", factor, sigma_three, precision=lax.Precision.HIGHEST), "pcol")
    own_part = jnp.einsum("nsr,nst->nrt", diag_inv, diag_inv, precision=lax.Precision.HIGHEST)
    return sigma, own_part - cross


def solution(mesh):
    in_specs = (
        P(("cfg", "prow"), "pcol"),
        P(("cfg", "pcol"), "prow"),
        P(("cfg", "prow"), None, None),
        P(("cfg", "prow"), None),
    )
    out_specs = (P(("cfg", "pcol"), "prow"), P(("cfg", "prow"), None, None))
    local = functools.partial(local_eight, mesh) if mesh.shape["prow"] == 8 else local_any
    return jax.shard_map(local, mesh=mesh, in_specs=in_specs, out_specs=out_specs, check_vma=False)
```

```python
import functools

import jax
import jax.numpy as jnp
from jax import lax
from jax.experimental import pallas as pl
from jax.experimental.pallas import tpu as pltpu
from jax.sharding import PartitionSpec as P

W = 1024
BLOCK_ROWS = 8
SPARE = 8
AXES = ("cfg", "prow", "pcol")
VMEM = pl.BlockSpec(memory_space=pltpu.VMEM)
SMEM = pl.BlockSpec(memory_space=pltpu.SMEM)


def split(value):
    high = value.astype(jnp.bfloat16)
    low = (value - high.astype(jnp.float32)).astype(jnp.bfloat16)
    return high, low


def product(left, right, dims):
    dot = functools.partial(lax.dot_general, dimension_numbers=(dims, ((), ())), preferred_element_type=jnp.float32)
    return dot(left[0], right[0]) + (dot(left[0], right[1]) + dot(left[1], right[0]))


PLAIN = ((1,), (0,))
FIRST = ((0,), (0,))


def factor_kernel(mask, panel, diag_inv, factor):
    children, width = diag_inv.shape[:2]
    here = mask.shape[0] // children
    block = panel.shape[0] // here
    for j in range(children):
        columns = pl.ds(j * width, width)
        masked = jnp.concatenate(
            [panel[pl.ds(r * block, block), columns] * mask[pl.ds(j * here + r, 1), :] for r in range(here)], axis=0
        )
        factor[:, columns] = product(split(masked), split(diag_inv[j]), PLAIN)


def own_place():
    prow = lax.axis_index("prow")
    return lax.rem(prow, 4), lax.div(prow, 4) == lax.axis_index("pcol")


def places(place):
    beside = place + 1 - 2 * lax.rem(place, 2)
    return beside, lax.rem(place + 2, 4), lax.rem(beside + 2, 4)


def at(place, block):
    return pl.ds(pl.multiple_of(place * block, block), block)


def parts(piece):
    block = piece.shape[1]
    half, last = block // 2, 2 * block
    return [piece.at[pl.ds(start, size)] for start, size in ((0, block), (block, half), (block + half, half), (last, SPARE))]


def folded(block):
    half = block.shape[0] // 2
    top, bottom = block[:half], block[half:]
    row, lane = (lax.broadcasted_iota(jnp.int32, top.shape, axis) for axis in (0, 1))
    top = jnp.where((lane < half) & (row > lane), pltpu.roll(bottom, half, 1), top)
    return top, jnp.sum(jnp.where(row == lane - half, bottom, 0.0), axis=0, keepdims=True)


def unfolded(top, ends):
    half = top.shape[0]
    row, lane = (lax.broadcasted_iota(jnp.int32, top.shape, axis) for axis in (0, 1))
    turned = jnp.concatenate([top, jnp.zeros_like(top)], axis=0).T
    upper = jnp.where((lane < half) & (row > lane), turned[:half], top)
    own = jnp.where(row < lane - half, pltpu.roll(turned[:half], half, 1), ends)
    own = jnp.where(row > lane - half, pltpu.roll(top, half, 1), own)
    return jnp.concatenate([upper, jnp.where(lane < half, turned[half:], own)], axis=0)


def pieces_kernel(
    sigma_top, pattern, panel, diag_inv, first, second, mask, panel_here, inverse_here, own, pattern_here, sems
):
    place, diagonal = own_place()
    loads = [
        pltpu.make_async_copy(source, here, sems.at[n])
        for n, (source, here) in enumerate(
            ((sigma_top, own), (pattern, pattern_here), (panel, panel_here), (diag_inv, inverse_here))
        )
    ]
    for load in loads:
        load.start()
    loads[0].wait()
    block = own.shape[0]
    half = block // 2

    @pl.when(diagonal)
    def _():
        opposite = at(lax.rem(place + 2, 4), block)
        top, ends = folded(own[:, at(place, block)])
        for piece in (first, second):
            following, _, folded_top, folded_ends = parts(piece)
            following[...] = own[:, at(lax.rem(place + 1, 4), block)]
            folded_top[...] = top
            folded_ends[...] = jnp.broadcast_to(ends, folded_ends.shape)

        @pl.when(place < 2)
        def _():
            for piece in (first, second):
                parts(piece)[1][...] = own[pl.ds(0, half), opposite]

        @pl.when(place >= 2)
        def _():
            turned = own[:, opposite].T
            for piece in (first, second):
                parts(piece)[1][...] = turned[half:]

    @pl.when(jnp.logical_not(diagonal))
    def _():
        for n, piece in enumerate((first, second)):
            for b in range(2):
                piece[pl.ds(b * block, block), :] = own[:, pl.ds((2 * n + b) * block, block)]
            piece[pl.ds(2 * block, SPARE), :] = jnp.zeros((SPARE, block), jnp.float32)

    loads[1].wait()
    core = lax.axis_index("pcol")
    here = mask.shape[0] // pattern.shape[0]
    for j in range(pattern.shape[0]):
        for r in range(here):
            kept = pattern_here[j, core * here + r].astype(jnp.float32)
            mask[pl.ds(j * here + r, 1), :] = jnp.full((1, mask.shape[1]), kept, jnp.float32)
    loads[2].wait()
    loads[3].wait()


def symmetric(quadrant, pieces):
    block = quadrant.shape[0] // 4
    half = block // 2
    for piece, place in pieces:
        rows = at(place, block)
        following, opposite, top, ends = piece
        quadrant[rows, at(place, block)] = unfolded(top[...], ends[pl.ds(0, 1), :])
        quadrant[rows, at(lax.rem(place + 1, 4), block)] = following[...]
        low = lax.rem(place, 2)
        quadrant[
            pl.ds(pl.multiple_of(low * block + lax.div(place, 2) * half, half), half), at(low + 2, block)
        ] = opposite[...]
    for row, column in ((0, 1), (1, 2), (2, 3), (3, 0), (0, 2), (1, 3)):
        rows, columns = pl.ds(row * block, block), pl.ds(column * block, block)
        quadrant[columns, rows] = quadrant[rows, columns].T


def row_blocks(quadrant, where, halves):
    block = quadrant.shape[0] // 4
    for n, piece in enumerate(halves):
        for b in range(2):
            quadrant[at(where, block), pl.ds((2 * n + b) * block, block)] = piece[pl.ds(b * block, block), :]


def own_half_kernel(mine_a, mine_b, got1, got2, got3, got4, got5, got6, far_high, far_low, quadrant, sent_a, sent_b):
    place, diagonal = own_place()
    beside, over, across = places(place)
    rows, block = sent_a.shape[0], quadrant.shape[0] // 4

    @pl.when(diagonal)
    def _():
        symmetric(
            quadrant,
            ((parts(mine_a), place), (parts(got3), beside), (parts(got4), over), (parts(got6), across)),
        )
        for n, piece in enumerate((got1, got5, got2)):
            rest = piece.shape[0] - rows
            sent_a[:, pl.ds(n * block, block)] = piece[pl.ds(0, rows), :]
            sent_a[pl.ds(n * rest, rest), pl.ds(3 * block, block)] = piece[pl.ds(rows, rest), :]

    @pl.when(jnp.logical_not(diagonal))
    def _():
        row_blocks(quadrant, place, (mine_a, mine_b))
        row_blocks(quadrant, beside, (got1, got4))
        row_blocks(quadrant, over, (got2, got3))
        row_blocks(quadrant, across, (got5, got6))
        result = product(split(quadrant[...]), (far_high[...], far_low[...]), PLAIN)
        sent_a[...] = result[:rows]
        sent_b[...] = result[rows:]


def columns_of(value, j, width):
    return tuple(part[:, j * width : (j + 1) * width] for part in value)


def split_kernel(factor, factor_other, diag_inv, far_high, far_low, turned_high, turned_low, own_part):
    _, diagonal = own_place()

    def write(rows):
        far_high[...], far_low[...] = split(rows)
        turned_high[...], turned_low[...] = split(rows.T)

    @pl.when(diagonal)
    def _():
        write(factor_other[...])

    @pl.when(jnp.logical_not(diagonal))
    def _():
        write(factor[...])

        for j in range(own_part.shape[0]):
            inverse = split(diag_inv[j])
            own_part[j] = product(inverse, inverse, FIRST)


def near_kernel(quadrant, factor, factor_other, turned_high, turned_low, own_part, partial, cross):
    _, diagonal = own_place()
    width = cross.shape[1]

    @pl.when(diagonal)
    def _():
        own = split(factor[...])
        partial[...] = product(split(quadrant[...]), own, PLAIN)
        value = split(partial[...])
        for j in range(cross.shape[0]):
            cross[j] = product(columns_of(own, j, width), columns_of(value, j, width), FIRST)

    @pl.when(jnp.logical_not(diagonal))
    def _():
        partial[...] = product(split(quadrant[...]), split(factor_other[...]), FIRST)
        value = split(partial[...])
        for j in range(cross.shape[0]):
            rows = pl.ds(j * width, width)
            mixed = product((turned_high[rows, :], turned_low[rows, :]), columns_of(value, j, width), PLAIN)
            cross[j] = own_part[j] + (mixed + mixed.T)


def again_kernel(got, same):
    same[...] = got[...]


def early_parts(early, block):
    half = block // 2
    return [
        [
            early.at[pl.ds(start, size), pl.ds(n * block, block)]
            for start, size in ((0, block), (block, half), (block + half, half))
        ]
        + [early.at[pl.ds(n * SPARE, SPARE), pl.ds(3 * block, block)]]
        for n in range(3)
    ]


def far_kernel(got1, got2, got5, got7, early, far_high, far_low, turned_high, turned_low, cross, first, quadrant):
    place, diagonal = own_place()
    beside, over, across = places(place)
    width = cross.shape[1]

    @pl.when(diagonal)
    def _():
        symmetric(
            quadrant,
            ((parts(got1), place), (parts(got2), over), (parts(got5), beside), (parts(got7), across)),
        )
        value = split(product(split(quadrant[...]), (far_high[...], far_low[...]), PLAIN))
        for j in range(cross.shape[0]):
            rows = pl.ds(j * width, width)
            cross[j] = product((turned_high[rows, :], turned_low[rows, :]), columns_of(value, j, width), PLAIN)

    @pl.when(jnp.logical_not(diagonal))
    def _():
        quadrant[...] = jnp.zeros_like(quadrant)
        symmetric(quadrant, zip(early_parts(early, got1.shape[1]), (place, beside, over)))
        first[...] = product(split(quadrant[...]), (far_high[...], far_low[...]), PLAIN)


def panel_kernel(
    early_a, early_b, late, partial, far_high, far_low, turned_high, turned_low, near, near_other, far, first,
    sigma, diag, total, sigma_here, diag_here, sigma_sems, diag_sems,
):
    place, diagonal = own_place()
    beside, over, across = places(place)
    width = diag.shape[1]
    children = range(diag.shape[0])
    chunk = sigma.shape[0] // sigma_sems.shape[0]
    chunks = [pl.ds(c * chunk, chunk) for c in range(sigma_sems.shape[0])]
    sigma_stores = [
        pltpu.make_async_copy(sigma_here.at[rows], sigma.at[rows], sigma_sems.at[c]) for c, rows in enumerate(chunks)
    ]
    diag_stores = [pltpu.make_async_copy(diag_here.at[j], diag.at[j], diag_sems.at[j]) for j in children]

    @pl.when(diagonal)
    def _():
        for j in children:
            diag_here[j] = (near[j] + near_other[j]) + far[j]
            diag_stores[j].start()
        early = [ref[pl.ds(c * chunk, chunk), :] for ref in (early_a, early_b) for c in range(ref.shape[0] // chunk)]
        for rows, store, here in zip(chunks, sigma_stores, early):
            sigma_here[rows, :] = -(partial[rows, :] + here)
            store.start()

    @pl.when(jnp.logical_not(diagonal))
    def _():
        block = late.shape[1]
        half = block // 2
        after, low = lax.rem(across + 1, 4), lax.rem(across, 2)
        piece_rows = pl.ds(pl.multiple_of(low * block + lax.div(across, 2) * half, half), half)

        def factors(rows):
            return far_high[rows, :], far_low[rows, :]

        following, opposite, top, ends = parts(late)
        own = split(unfolded(top[...], ends[pl.ds(0, 1), :]))
        following, opposite = split(following[...]), split(opposite[...])
        total[...] = first[...]
        total[at(across, block), :] += product(own, factors(at(across, block)), PLAIN) + product(
            following, factors(at(after, block)), PLAIN
        )
        total[at(after, block), :] += product(following, factors(at(across, block)), FIRST)
        total[piece_rows, :] += product(opposite, factors(at(low + 2, block)), PLAIN)
        total[at(low + 2, block), :] += product(opposite, factors(piece_rows), FIRST)
        values = []
        for rows, store in zip(chunks, sigma_stores):
            last = total[rows, :]
            sigma_here[rows, :] = -(partial[rows, :] + last)
            store.start()
            values.append(split(last))
        value = tuple(jnp.concatenate(rows, axis=0) for rows in zip(*values))
        for j in children:
            turned = pl.ds(j * width, width)
            inner = product((turned_high[turned, :], turned_low[turned, :]), columns_of(value, j, width), PLAIN)
            diag_here[j] = (near[j] + near_other[j]) + inner
            diag_stores[j].start()

    for store in (*sigma_stores, *diag_stores):
        store.wait()


def call(kernel, out_shapes, flops, *args, specs=None, out_specs=None, scratch=()):
    moved = sum(a.size * a.dtype.itemsize for a in (*args, *out_shapes))
    return pl.pallas_call(
        kernel,
        out_shape=out_shapes,
        in_specs=specs or [VMEM] * len(args),
        out_specs=out_specs or [VMEM] * len(out_shapes),
        scratch_shapes=scratch,
        cost_estimate=pl.CostEstimate(flops=flops, bytes_accessed=moved, transcendentals=0),
        compiler_params=pltpu.CompilerParams(vmem_limit_bytes=32 * 1024 * 1024),
    )(*args)


def permute(value, mesh, diagonal_step, other_step=None):
    cfgs, prows, cores = (mesh.shape[axis] for axis in AXES)
    pairs = []
    for c in range(cfgs):
        for p in range(prows):
            for k in range(cores):
                step = diagonal_step if p // 4 == k else other_step
                to_cfg, to = (cfgs - 1 - c, p) if step is None else (c, p ^ step)
                pairs.append(((c * prows + p) * cores + k, (to_cfg * prows + to) * cores + (k ^ (p // 4) ^ (to // 4))))
    return lax.ppermute(value, AXES, pairs)


def exchange(value, mesh):
    cfgs, prows, cores = (mesh.shape[axis] for axis in AXES)
    return lax.ppermute(value, AXES, [(d, d ^ 1) for d in range(cfgs * prows * cores)])


def local_eight(mesh, sigma_top, panel_l, diag_inv, pattern):
    f32 = jnp.float32
    half_rows, own_columns = panel_l.shape
    block = sigma_top.shape[0]
    local_sn, width = diag_inv.shape[:2]
    shape = lambda *dims: jax.ShapeDtypeStruct(dims, f32)
    size = 2 * block + SPARE
    panel, square = shape(half_rows, own_columns), shape(half_rows, half_rows)
    children = shape(*diag_inv.shape)
    halves = [jax.ShapeDtypeStruct((half_rows, own_columns), jnp.bfloat16)] * 2
    turned = [jax.ShapeDtypeStruct((own_columns, half_rows), jnp.bfloat16)] * 2
    anywhere = pl.BlockSpec(memory_space=pl.ANY)
    in_hbm = lambda value: pltpu.with_memory_space_constraint(value, pltpu.HBM)
    step = 2 * half_rows * half_rows * own_columns
    mine_a, mine_b, mask, panel_here, inverse_here = call(
        pieces_kernel,
        [shape(size, block)] * 2 + [shape(local_sn * (half_rows // block), width), panel, children],
        1,
        in_hbm(sigma_top),
        in_hbm(pattern),
        in_hbm(panel_l),
        in_hbm(diag_inv),
        specs=[anywhere] * 4,
        scratch=[
            pltpu.VMEM(sigma_top.shape, f32),
            pltpu.SMEM(pattern.shape, jnp.int32),
            pltpu.SemaphoreType.DMA((4,)),
        ],
    )
    got1 = permute(mine_a, mesh, 4, 1)
    got2 = permute(mine_a, mesh, 6, 2)
    got3 = permute(mine_b, mesh, 1, 2)
    got4 = permute(mine_b, mesh, 2, 1)
    got5 = permute(got1, mesh, 1, 2)
    got6 = permute(got4, mesh, 1, 2)
    (got2_again,) = call(again_kernel, [shape(size, block)], 40 * step, got2)
    got7 = permute(got2_again, mesh, 1)
    (got7,) = call(again_kernel, [shape(size, block)], 16 * step, got7)
    (factor,) = call(
        factor_kernel,
        [panel],
        1,
        mask,
        panel_here,
        inverse_here,
    )
    factor_other = exchange(factor, mesh)
    *far_rows, own_part = call(split_kernel, [*halves, *turned, children], 1, factor, factor_other, inverse_here)
    own_half, sent_a, sent_b = call(
        own_half_kernel,
        [square] + [shape(half_rows // 2, own_columns)] * 2,
        36 * step,
        mine_a, mine_b, got1, got2, got3, got4, got5, got6, *far_rows[:2],
    )
    early_a, early_b = exchange(sent_a, mesh), exchange(sent_b, mesh)
    partial, near = call(near_kernel, [panel, children], 1, own_half, factor, factor_other, *far_rows[2:], own_part)
    near_other = exchange(near, mesh)
    late = exchange(got7, mesh)
    far, first = call(
        far_kernel,
        [children, panel],
        1,
        got1, got2, got5, got7, early_a, *far_rows,
        scratch=[pltpu.VMEM(square.shape, f32)],
    )
    return tuple(
        call(
            panel_kernel,
            [panel, children],
            1,
            early_a, early_b, late, partial, *far_rows, near, near_other, far, first,
            out_specs=[anywhere] * 2,
            scratch=[
                pltpu.VMEM(square.shape, f32),
                pltpu.VMEM(panel.shape, f32),
                pltpu.VMEM(children.shape, f32),
                pltpu.SemaphoreType.DMA((half_rows // block,)),
                pltpu.SemaphoreType.DMA((local_sn,)),
            ],
        )
    )


def local_any(sigma_top, panel_l, diag_inv, pattern):
    half_rows = panel_l.shape[0]
    local_sn, width = diag_inv.shape[:2]
    row_mask = jnp.repeat(pattern.astype(jnp.float32), W // BLOCK_ROWS, axis=1)
    row_mask = lax.dynamic_slice_in_dim(row_mask, lax.axis_index("pcol") * half_rows, half_rows, 1)
    masked = panel_l.reshape(half_rows, local_sn, width) * jnp.transpose(row_mask)[:, :, None]
    factor = jnp.einsum("wns,nst->wnt", masked, diag_inv, precision=lax.Precision.HIGHEST)
    factor_flat = factor.reshape(half_rows, local_sn * width)
    whole = lax.all_gather(factor_flat, "pcol", axis=0, tiled=True)
    gathered = lax.all_gather(sigma_top, "prow", axis=0, tiled=True)
    sigma = -jnp.einsum("wv,wt->vt", gathered, whole, precision=lax.Precision.HIGHEST)
    sigma_three = sigma.reshape(half_rows, local_sn, width)
    cross = lax.psum(jnp.einsum("wnr,wnt->nrt", factor, sigma_three, precision=lax.Precision.HIGHEST), "pcol")
    own_part = jnp.einsum("nsr,nst->nrt", diag_inv, diag_inv, precision=lax.Precision.HIGHEST)
    return sigma, own_part - cross


def solution(mesh):
    in_specs = (
        P(("cfg", "prow"), "pcol"),
        P(("cfg", "pcol"), "prow"),
        P(("cfg", "prow"), None, None),
        P(("cfg", "prow"), None),
    )
    out_specs = (P(("cfg", "pcol"), "prow"), P(("cfg", "prow"), None, None))
    local = functools.partial(local_eight, mesh) if mesh.shape["prow"] == 8 else local_any
    return jax.shard_map(local, mesh=mesh, in_specs=in_specs, out_specs=out_specs, check_vma=False)
```

```python
import functools

import jax
import jax.numpy as jnp
from jax import lax
from jax.experimental import pallas as pl
from jax.experimental.pallas import tpu as pltpu
from jax.sharding import PartitionSpec as P

W = 1024
BLOCK_ROWS = 8
SPARE = 8
AXES = ("cfg", "prow", "pcol")
VMEM = pl.BlockSpec(memory_space=pltpu.VMEM)
SMEM = pl.BlockSpec(memory_space=pltpu.SMEM)


def split(value):
    high = value.astype(jnp.bfloat16)
    low = (value - high.astype(jnp.float32)).astype(jnp.bfloat16)
    return high, low


def product(left, right, dims):
    dot = functools.partial(lax.dot_general, dimension_numbers=(dims, ((), ())), preferred_element_type=jnp.float32)
    return dot(left[0], right[0]) + (dot(left[0], right[1]) + dot(left[1], right[0]))


PLAIN = ((1,), (0,))
FIRST = ((0,), (0,))


def factor_kernel(mask, panel, diag_inv, factor):
    children, width = diag_inv.shape[:2]
    here = mask.shape[0] // children
    block = panel.shape[0] // here
    for j in range(children):
        columns = pl.ds(j * width, width)
        masked = jnp.concatenate(
            [panel[pl.ds(r * block, block), columns] * mask[pl.ds(j * here + r, 1), :] for r in range(here)], axis=0
        )
        factor[:, columns] = product(split(masked), split(diag_inv[j]), PLAIN)


def own_place():
    prow = lax.axis_index("prow")
    return lax.rem(prow, 4), lax.div(prow, 4) == lax.axis_index("pcol")


def places(place):
    beside = place + 1 - 2 * lax.rem(place, 2)
    return beside, lax.rem(place + 2, 4), lax.rem(beside + 2, 4)


def at(place, block):
    return pl.ds(pl.multiple_of(place * block, block), block)


def parts(piece):
    block = piece.shape[1]
    half, last = block // 2, 2 * block
    return [piece.at[pl.ds(start, size)] for start, size in ((0, block), (block, half), (block + half, half), (last, SPARE))]


def folded(block):
    half = block.shape[0] // 2
    top, bottom = block[:half], block[half:]
    row, lane = (lax.broadcasted_iota(jnp.int32, top.shape, axis) for axis in (0, 1))
    top = jnp.where((lane < half) & (row > lane), pltpu.roll(bottom, half, 1), top)
    return top, jnp.sum(jnp.where(row == lane - half, bottom, 0.0), axis=0, keepdims=True)


def unfolded(top, ends):
    half = top.shape[0]
    row, lane = (lax.broadcasted_iota(jnp.int32, top.shape, axis) for axis in (0, 1))
    turned = jnp.concatenate([top, jnp.zeros_like(top)], axis=0).T
    upper = jnp.where((lane < half) & (row > lane), turned[:half], top)
    own = jnp.where(row < lane - half, pltpu.roll(turned[:half], half, 1), ends)
    own = jnp.where(row > lane - half, pltpu.roll(top, half, 1), own)
    return jnp.concatenate([upper, jnp.where(lane < half, turned[half:], own)], axis=0)


def pieces_kernel(sigma_top, pattern, first, second, mask, own, pattern_here, sems):
    place, diagonal = own_place()
    loads = [
        pltpu.make_async_copy(source, here, sems.at[n])
        for n, (source, here) in enumerate(
            ((sigma_top, own), (pattern, pattern_here))
        )
    ]
    for load in loads:
        load.start()
    loads[0].wait()
    block = own.shape[0]
    half = block // 2

    @pl.when(diagonal)
    def _():
        opposite = at(lax.rem(place + 2, 4), block)
        top, ends = folded(own[:, at(place, block)])
        for piece in (first, second):
            following, _, folded_top, folded_ends = parts(piece)
            following[...] = own[:, at(lax.rem(place + 1, 4), block)]
            folded_top[...] = top
            folded_ends[...] = jnp.broadcast_to(ends, folded_ends.shape)

        @pl.when(place < 2)
        def _():
            for piece in (first, second):
                parts(piece)[1][...] = own[pl.ds(0, half), opposite]

        @pl.when(place >= 2)
        def _():
            turned = own[:, opposite].T
            for piece in (first, second):
                parts(piece)[1][...] = turned[half:]

    @pl.when(jnp.logical_not(diagonal))
    def _():
        for n, piece in enumerate((first, second)):
            for b in range(2):
                piece[pl.ds(b * block, block), :] = own[:, pl.ds((2 * n + b) * block, block)]
            piece[pl.ds(2 * block, SPARE), :] = jnp.zeros((SPARE, block), jnp.float32)

    loads[1].wait()
    core = lax.axis_index("pcol")
    here = mask.shape[0] // pattern.shape[0]
    for j in range(pattern.shape[0]):
        for r in range(here):
            kept = pattern_here[j, core * here + r].astype(jnp.float32)
            mask[pl.ds(j * here + r, 1), :] = jnp.full((1, mask.shape[1]), kept, jnp.float32)


def symmetric(quadrant, pieces):
    block = quadrant.shape[0] // 4
    half = block // 2
    for piece, place in pieces:
        rows = at(place, block)
        following, opposite, top, ends = piece
        quadrant[rows, at(place, block)] = unfolded(top[...], ends[pl.ds(0, 1), :])
        quadrant[rows, at(lax.rem(place + 1, 4), block)] = following[...]
        low = lax.rem(place, 2)
        quadrant[
            pl.ds(pl.multiple_of(low * block + lax.div(place, 2) * half, half), half), at(low + 2, block)
        ] = opposite[...]
    for row, column in ((0, 1), (1, 2), (2, 3), (3, 0), (0, 2), (1, 3)):
        rows, columns = pl.ds(row * block, block), pl.ds(column * block, block)
        quadrant[columns, rows] = quadrant[rows, columns].T


def row_blocks(quadrant, where, halves):
    block = quadrant.shape[0] // 4
    for n, piece in enumerate(halves):
        for b in range(2):
            quadrant[at(where, block), pl.ds((2 * n + b) * block, block)] = piece[pl.ds(b * block, block), :]


def own_half_kernel(mine_a, got1, got2, got3, got4, got5, got6, products, far_high, far_low, quadrant, sent_a, sent_b):
    place, diagonal = own_place()
    beside, over, across = places(place)
    rows, block = sent_a.shape[0], quadrant.shape[0] // 4

    @pl.when(diagonal)
    def _():
        symmetric(
            quadrant,
            ((parts(mine_a), place), (parts(got3), beside), (parts(got4), over), (parts(got6), across)),
        )
        for n, piece in enumerate((got1, got5, got2)):
            rest = piece.shape[0] - rows
            sent_a[:, pl.ds(n * block, block)] = piece[pl.ds(0, rows), :]
            sent_a[pl.ds(n * rest, rest), pl.ds(3 * block, block)] = piece[pl.ds(rows, rest), :]

    @pl.when(jnp.logical_not(diagonal))
    def _():
        last = product(split(row_of(got5, got6)), (far_high[...], far_low[...]), PLAIN)
        sent_a[...] = products[pl.ds(0, rows), :]
        sent_b[pl.ds(0, block), :] = products[pl.ds(rows, block), :]
        sent_b[pl.ds(block, block), :] = last


def columns_of(value, j, width):
    return tuple(part[:, j * width : (j + 1) * width] for part in value)


def row_of(first, second):
    block = first.shape[1]
    return jnp.concatenate([piece[pl.ds(b * block, block), :] for piece in (first, second) for b in range(2)], axis=1)


def prepare_kernel(
    mine_a, mine_b, got1, got2, got3, got4, factor, factor_other, diag_inv,
    far_high, far_low, turned_high, turned_low, own_part, products, partial,
):
    place, diagonal = own_place()
    beside, over, _ = places(place)
    block = mine_a.shape[1]

    def write(rows):
        far_high[...], far_low[...] = split(rows)
        turned_high[...], turned_low[...] = split(rows.T)

    @pl.when(diagonal)
    def _():
        write(factor_other[...])

    @pl.when(jnp.logical_not(diagonal))
    def _():
        write(factor[...])
        for j in range(own_part.shape[0]):
            inverse = split(diag_inv[j])
            own_part[j] = product(inverse, inverse, FIRST)
        rows = split(jnp.concatenate([row_of(mine_a, mine_b), row_of(got1, got4), row_of(got2, got3)], axis=0))
        products[...] = product(rows, (far_high[...], far_low[...]), PLAIN)
        factors = jnp.concatenate([factor_other[at(where, block), :] for where in (place, beside, over)], axis=0)
        partial[...] = product(rows, split(factors), FIRST)


def near_kernel(
    quadrant, got5, got6, most, factor, factor_other, turned_high, turned_low, own_part, partial, cross
):
    place, diagonal = own_place()
    across = places(place)[2]
    width = cross.shape[1]

    @pl.when(diagonal)
    def _():
        own = split(factor[...])
        partial[...] = product(split(quadrant[...]), own, PLAIN)
        value = split(partial[...])
        for j in range(cross.shape[0]):
            cross[j] = product(columns_of(own, j, width), columns_of(value, j, width), FIRST)

    @pl.when(jnp.logical_not(diagonal))
    def _():
        factors = split(factor_other[at(across, got5.shape[1]), :])
        partial[...] = most[...] + product(split(row_of(got5, got6)), factors, FIRST)
        value = split(partial[...])
        for j in range(cross.shape[0]):
            rows = pl.ds(j * width, width)
            mixed = product((turned_high[rows, :], turned_low[rows, :]), columns_of(value, j, width), PLAIN)
            cross[j] = own_part[j] + (mixed + mixed.T)


def again_kernel(got, same):
    same[...] = got[...]


def joined(left, right, dims):
    (over,), (under,) = dims
    return lax.dot_general(
        jnp.concatenate([left[0], left[0], left[1]], axis=over),
        jnp.concatenate([right[0], right[1], right[0]], axis=under),
        (dims, ((), ())),
        preferred_element_type=jnp.float32,
    )


def early_parts(early, block):
    half = block // 2
    return [
        [
            early.at[pl.ds(start, size), pl.ds(n * block, block)]
            for start, size in ((0, block), (block, half), (block + half, half))
        ]
        + [early.at[pl.ds(n * SPARE, SPARE), pl.ds(3 * block, block)]]
        for n in range(3)
    ]


def far_kernel(got1, got2, got5, got7, early, far_high, far_low, turned_high, turned_low, cross, first, quadrant):
    place, diagonal = own_place()
    beside, over, across = places(place)
    width = cross.shape[1]

    @pl.when(diagonal)
    def _():
        symmetric(
            quadrant,
            ((parts(got1), place), (parts(got2), over), (parts(got5), beside), (parts(got7), across)),
        )
        value = split(product(split(quadrant[...]), (far_high[...], far_low[...]), PLAIN))
        for j in range(cross.shape[0]):
            rows = pl.ds(j * width, width)
            cross[j] = product((turned_high[rows, :], turned_low[rows, :]), columns_of(value, j, width), PLAIN)

    @pl.when(jnp.logical_not(diagonal))
    def _():
        quadrant[...] = jnp.zeros_like(quadrant)
        symmetric(quadrant, zip(early_parts(early, got1.shape[1]), (place, beside, over)))
        first[...] = product(split(quadrant[...]), (far_high[...], far_low[...]), PLAIN)


def panel_kernel(
    early_a, early_b, late, partial, far_high, far_low, turned_high, turned_low, near, near_other, far, first,
    sigma, diag, total, sigma_here, diag_here, sigma_sems, diag_sems,
):
    place, diagonal = own_place()
    beside, over, across = places(place)
    width = diag.shape[1]
    children = range(diag.shape[0])
    chunk = sigma.shape[0] // sigma_sems.shape[0]
    chunks = [pl.ds(c * chunk, chunk) for c in range(sigma_sems.shape[0])]

    def store(rows, c):
        return pltpu.make_async_copy(sigma_here.at[rows], sigma.at[rows], sigma_sems.at[c])

    diag_stores = [pltpu.make_async_copy(diag_here.at[j], diag.at[j], diag_sems.at[j]) for j in children]

    @pl.when(diagonal)
    def _():
        for j in children:
            diag_here[j] = (near[j] + near_other[j]) + far[j]
            diag_stores[j].start()
        early = [ref[pl.ds(c * chunk, chunk), :] for ref in (early_a, early_b) for c in range(ref.shape[0] // chunk)]
        for n, here in enumerate(early):
            rows = at((place, beside, over, across)[n], chunk)
            sigma_here[rows, :] = -(partial[rows, :] + here)
            store(rows, n).start()

    @pl.when(jnp.logical_not(diagonal))
    def _():
        block = late.shape[1]
        half = block // 2
        after, low = lax.rem(across + 1, 4), lax.rem(across, 2)
        piece_rows = pl.ds(pl.multiple_of(low * block + lax.div(across, 2) * half, half), half)

        def factors(rows):
            return far_high[rows, :], far_low[rows, :]

        following, opposite, top, ends = parts(late)
        own = split(unfolded(top[...], ends[pl.ds(0, 1), :]))
        following, opposite = split(following[...]), split(opposite[...])
        total[...] = first[...]
        total[at(across, block), :] += joined(own, factors(at(across, block)), PLAIN) + joined(
            following, factors(at(after, block)), PLAIN
        )
        total[at(after, block), :] += joined(following, factors(at(across, block)), FIRST)
        total[piece_rows, :] += joined(opposite, factors(at(low + 2, block)), PLAIN)
        total[at(low + 2, block), :] += joined(opposite, factors(piece_rows), FIRST)
        values = []
        for c, rows in enumerate(chunks):
            last = total[rows, :]
            sigma_here[rows, :] = -(partial[rows, :] + last)
            store(rows, c).start()
            values.append(split(last))
        value = tuple(jnp.concatenate(rows, axis=0) for rows in zip(*values))
        for j in children:
            turned = pl.ds(j * width, width)
            inner = product((turned_high[turned, :], turned_low[turned, :]), columns_of(value, j, width), PLAIN)
            diag_here[j] = (near[j] + near_other[j]) + inner
            diag_stores[j].start()

    for copy in (*(store(rows, c) for c, rows in enumerate(chunks)), *diag_stores):
        copy.wait()


def call(kernel, out_shapes, flops, *args, specs=None, out_specs=None, scratch=()):
    moved = sum(a.size * a.dtype.itemsize for a in (*args, *out_shapes))
    return pl.pallas_call(
        kernel,
        out_shape=out_shapes,
        in_specs=specs or [VMEM] * len(args),
        out_specs=out_specs or [VMEM] * len(out_shapes),
        scratch_shapes=scratch,
        cost_estimate=pl.CostEstimate(flops=flops, bytes_accessed=moved, transcendentals=0),
        compiler_params=pltpu.CompilerParams(vmem_limit_bytes=32 * 1024 * 1024),
    )(*args)


def permute(value, mesh, diagonal_step, other_step=None):
    cfgs, prows, cores = (mesh.shape[axis] for axis in AXES)
    pairs = []
    for c in range(cfgs):
        for p in range(prows):
            for k in range(cores):
                step = diagonal_step if p // 4 == k else other_step
                to_cfg, to = (cfgs - 1 - c, p) if step is None else (c, p ^ step)
                pairs.append(((c * prows + p) * cores + k, (to_cfg * prows + to) * cores + (k ^ (p // 4) ^ (to // 4))))
    return lax.ppermute(value, AXES, pairs)


def exchange(value, mesh):
    cfgs, prows, cores = (mesh.shape[axis] for axis in AXES)
    return lax.ppermute(value, AXES, [(d, d ^ 1) for d in range(cfgs * prows * cores)])


def local_eight(mesh, sigma_top, panel_l, diag_inv, pattern):
    f32 = jnp.float32
    half_rows, own_columns = panel_l.shape
    block = sigma_top.shape[0]
    local_sn, width = diag_inv.shape[:2]
    shape = lambda *dims: jax.ShapeDtypeStruct(dims, f32)
    size = 2 * block + SPARE
    panel, square = shape(half_rows, own_columns), shape(half_rows, half_rows)
    children = shape(*diag_inv.shape)
    halves = [jax.ShapeDtypeStruct((half_rows, own_columns), jnp.bfloat16)] * 2
    turned = [jax.ShapeDtypeStruct((own_columns, half_rows), jnp.bfloat16)] * 2
    anywhere = pl.BlockSpec(memory_space=pl.ANY)
    in_hbm = lambda value: pltpu.with_memory_space_constraint(value, pltpu.HBM)
    step = 2 * half_rows * half_rows * own_columns
    mine_a, mine_b, mask = call(
        pieces_kernel,
        [shape(size, block)] * 2 + [shape(local_sn * (half_rows // block), width)],
        40 * step,
        in_hbm(sigma_top),
        in_hbm(pattern),
        specs=[anywhere] * 2,
        scratch=[
            pltpu.VMEM(sigma_top.shape, f32),
            pltpu.SMEM(pattern.shape, jnp.int32),
            pltpu.SemaphoreType.DMA((2,)),
        ],
    )
    got1 = permute(mine_a, mesh, 4, 1)
    got2 = permute(mine_a, mesh, 6, 2)
    got3 = permute(mine_b, mesh, 1, 2)
    got4 = permute(mine_b, mesh, 2, 1)
    got5 = permute(got1, mesh, 1, 2)
    got6 = permute(got4, mesh, 1, 2)
    (got2_again,) = call(again_kernel, [shape(size, block)], 40 * step, got2)
    got7 = permute(got2_again, mesh, 1)
    (got7,) = call(again_kernel, [shape(size, block)], 16 * step, got7)
    (factor,) = call(
        factor_kernel,
        [panel],
        1,
        mask,
        panel_l,
        diag_inv,
    )
    factor_other = exchange(factor, mesh)
    *far_rows, own_part, products, most = call(
        prepare_kernel,
        [*halves, *turned, children, shape(3 * block, own_columns), panel],
        1,
        mine_a, mine_b, got1, got2, got3, got4, factor, factor_other, diag_inv,
    )
    own_half, sent_a, sent_b = call(
        own_half_kernel,
        [square] + [shape(half_rows // 2, own_columns)] * 2,
        36 * step,
        mine_a, got1, got2, got3, got4, got5, got6, products, *far_rows[:2],
    )
    early_a, early_b = exchange(sent_a, mesh), exchange(sent_b, mesh)
    partial, near = call(
        near_kernel,
        [panel, children],
        4 * step,
        own_half, got5, got6, most, factor, factor_other, *far_rows[2:], own_part,
    )
    near_other = exchange(near, mesh)
    late = exchange(got7, mesh)
    far, first = call(
        far_kernel,
        [children, panel],
        1,
        got1, got2, got5, got7, early_a, *far_rows,
        scratch=[pltpu.VMEM(square.shape, f32)],
    )
    return tuple(
        call(
            panel_kernel,
            [panel, children],
            1,
            early_a, early_b, late, partial, *far_rows, near, near_other, far, first,
            out_specs=[anywhere] * 2,
            scratch=[
                pltpu.VMEM(square.shape, f32),
                pltpu.VMEM(panel.shape, f32),
                pltpu.VMEM(children.shape, f32),
                pltpu.SemaphoreType.DMA((half_rows // block,)),
                pltpu.SemaphoreType.DMA((local_sn,)),
            ],
        )
    )


def local_any(sigma_top, panel_l, diag_inv, pattern):
    half_rows = panel_l.shape[0]
    local_sn, width = diag_inv.shape[:2]
    row_mask = jnp.repeat(pattern.astype(jnp.float32), W // BLOCK_ROWS, axis=1)
    row_mask = lax.dynamic_slice_in_dim(row_mask, lax.axis_index("pcol") * half_rows, half_rows, 1)
    masked = panel_l.reshape(half_rows, local_sn, width) * jnp.transpose(row_mask)[:, :, None]
    factor = jnp.einsum("wns,nst->wnt", masked, diag_inv, precision=lax.Precision.HIGHEST)
    factor_flat = factor.reshape(half_rows, local_sn * width)
    whole = lax.all_gather(factor_flat, "pcol", axis=0, tiled=True)
    gathered = lax.all_gather(sigma_top, "prow", axis=0, tiled=True)
    sigma = -jnp.einsum("wv,wt->vt", gathered, whole, precision=lax.Precision.HIGHEST)
    sigma_three = sigma.reshape(half_rows, local_sn, width)
    cross = lax.psum(jnp.einsum("wnr,wnt->nrt", factor, sigma_three, precision=lax.Precision.HIGHEST), "pcol")
    own_part = jnp.einsum("nsr,nst->nrt", diag_inv, diag_inv, precision=lax.Precision.HIGHEST)
    return sigma, own_part - cross


def solution(mesh):
    in_specs = (
        P(("cfg", "prow"), "pcol"),
        P(("cfg", "pcol"), "prow"),
        P(("cfg", "prow"), None, None),
        P(("cfg", "prow"), None),
    )
    out_specs = (P(("cfg", "pcol"), "prow"), P(("cfg", "prow"), None, None))
    local = functools.partial(local_eight, mesh) if mesh.shape["prow"] == 8 else local_any
    return jax.shard_map(local, mesh=mesh, in_specs=in_specs, out_specs=out_specs, check_vma=False)
```

```python
import functools

import jax
import jax.numpy as jnp
from jax import lax
from jax.experimental import pallas as pl
from jax.experimental.pallas import tpu as pltpu
from jax.sharding import PartitionSpec as P

W = 1024
BLOCK_ROWS = 8
SPARE = 8
AXES = ("cfg", "prow", "pcol")
VMEM = pl.BlockSpec(memory_space=pltpu.VMEM)
SMEM = pl.BlockSpec(memory_space=pltpu.SMEM)


def split(value):
    high = value.astype(jnp.bfloat16)
    low = (value - high.astype(jnp.float32)).astype(jnp.bfloat16)
    return high, low


def product(left, right, dims):
    dot = functools.partial(lax.dot_general, dimension_numbers=(dims, ((), ())), preferred_element_type=jnp.float32)
    return dot(left[0], right[0]) + (dot(left[0], right[1]) + dot(left[1], right[0]))


PLAIN = ((1,), (0,))
FIRST = ((0,), (0,))


def factor_kernel(mask, panel, diag_inv, factor, own_high, own_low):
    children, width = diag_inv.shape[:2]
    here = mask.shape[0] // children
    block = panel.shape[0] // here
    for j in range(children):
        columns = pl.ds(j * width, width)
        masked = jnp.concatenate(
            [panel[pl.ds(r * block, block), columns] * mask[pl.ds(j * here + r, 1), :] for r in range(here)], axis=0
        )
        rows = product(split(masked), split(diag_inv[j]), PLAIN)
        factor[:, columns] = rows
        own_high[:, columns], own_low[:, columns] = split(rows)


def own_place():
    prow = lax.axis_index("prow")
    return lax.rem(prow, 4), lax.div(prow, 4) == lax.axis_index("pcol")


def places(place):
    beside = place + 1 - 2 * lax.rem(place, 2)
    return beside, lax.rem(place + 2, 4), lax.rem(beside + 2, 4)


def at(place, block):
    return pl.ds(pl.multiple_of(place * block, block), block)


def parts(piece):
    block = piece.shape[1]
    half, last = block // 2, 2 * block
    return [piece.at[pl.ds(start, size)] for start, size in ((0, block), (block, half), (block + half, half), (last, SPARE))]


def folded(block):
    half = block.shape[0] // 2
    top, bottom = block[:half], block[half:]
    row, lane = (lax.broadcasted_iota(jnp.int32, top.shape, axis) for axis in (0, 1))
    top = jnp.where((lane < half) & (row > lane), pltpu.roll(bottom, half, 1), top)
    return top, jnp.sum(jnp.where(row == lane - half, bottom, 0.0), axis=0, keepdims=True)


def unfolded(top, ends):
    half = top.shape[0]
    row, lane = (lax.broadcasted_iota(jnp.int32, top.shape, axis) for axis in (0, 1))
    turned = jnp.concatenate([top, jnp.zeros_like(top)], axis=0).T
    upper = jnp.where((lane < half) & (row > lane), turned[:half], top)
    own = jnp.where(row < lane - half, pltpu.roll(turned[:half], half, 1), ends)
    own = jnp.where(row > lane - half, pltpu.roll(top, half, 1), own)
    return jnp.concatenate([upper, jnp.where(lane < half, turned[half:], own)], axis=0)


def pieces_kernel(sigma_top, pattern, first, second, mask, own, pattern_here, sems):
    place, diagonal = own_place()
    loads = [
        pltpu.make_async_copy(source, here, sems.at[n])
        for n, (source, here) in enumerate(
            ((sigma_top, own), (pattern, pattern_here))
        )
    ]
    for load in loads:
        load.start()
    loads[0].wait()
    block = own.shape[0]
    half = block // 2

    @pl.when(diagonal)
    def _():
        opposite = at(lax.rem(place + 2, 4), block)
        top, ends = folded(own[:, at(place, block)])
        for piece in (first, second):
            following, _, folded_top, folded_ends = parts(piece)
            following[...] = own[:, at(lax.rem(place + 1, 4), block)]
            folded_top[...] = top
            folded_ends[...] = jnp.broadcast_to(ends, folded_ends.shape)

        @pl.when(place < 2)
        def _():
            for piece in (first, second):
                parts(piece)[1][...] = own[pl.ds(0, half), opposite]

        @pl.when(place >= 2)
        def _():
            turned = own[:, opposite].T
            for piece in (first, second):
                parts(piece)[1][...] = turned[half:]

    @pl.when(jnp.logical_not(diagonal))
    def _():
        for n, piece in enumerate((first, second)):
            for b in range(2):
                piece[pl.ds(b * block, block), :] = own[:, pl.ds((2 * n + b) * block, block)]
            piece[pl.ds(2 * block, SPARE), :] = jnp.zeros((SPARE, block), jnp.float32)

    loads[1].wait()
    core = lax.axis_index("pcol")
    here = mask.shape[0] // pattern.shape[0]
    for j in range(pattern.shape[0]):
        for r in range(here):
            kept = pattern_here[j, core * here + r].astype(jnp.float32)
            mask[pl.ds(j * here + r, 1), :] = jnp.full((1, mask.shape[1]), kept, jnp.float32)


def symmetric(quadrant, pieces):
    block = quadrant.shape[0] // 4
    half = block // 2
    for piece, place in pieces:
        rows = at(place, block)
        following, opposite, top, ends = piece
        quadrant[rows, at(place, block)] = unfolded(top[...], ends[pl.ds(0, 1), :])
        quadrant[rows, at(lax.rem(place + 1, 4), block)] = following[...]
        low = lax.rem(place, 2)
        quadrant[
            pl.ds(pl.multiple_of(low * block + lax.div(place, 2) * half, half), half), at(low + 2, block)
        ] = opposite[...]
    for row, column in ((0, 1), (1, 2), (2, 3), (3, 0), (0, 2), (1, 3)):
        rows, columns = pl.ds(row * block, block), pl.ds(column * block, block)
        quadrant[columns, rows] = quadrant[rows, columns].T


def row_blocks(quadrant, where, halves):
    block = quadrant.shape[0] // 4
    for n, piece in enumerate(halves):
        for b in range(2):
            quadrant[at(where, block), pl.ds((2 * n + b) * block, block)] = piece[pl.ds(b * block, block), :]


def own_half_kernel(mine_a, got1, got2, got3, got4, got5, got6, products, far_high, far_low, quadrant, sent_a, sent_b):
    place, diagonal = own_place()
    beside, over, across = places(place)
    rows, block = sent_a.shape[0], quadrant.shape[0] // 4

    @pl.when(diagonal)
    def _():
        symmetric(
            quadrant,
            ((parts(mine_a), place), (parts(got3), beside), (parts(got4), over), (parts(got6), across)),
        )
        for n, piece in enumerate((got1, got5, got2)):
            rest = piece.shape[0] - rows
            sent_a[:, pl.ds(n * block, block)] = piece[pl.ds(0, rows), :]
            sent_a[pl.ds(n * rest, rest), pl.ds(3 * block, block)] = piece[pl.ds(rows, rest), :]

    @pl.when(jnp.logical_not(diagonal))
    def _():
        last = joined(split(row_of(got5, got6)), (far_high[...], far_low[...]), PLAIN)
        sent_a[...] = products[pl.ds(0, rows), :]
        sent_b[pl.ds(0, block), :] = products[pl.ds(rows, block), :]
        sent_b[pl.ds(block, block), :] = last


def columns_of(value, j, width):
    return tuple(part[:, j * width : (j + 1) * width] for part in value)


def row_of(first, second):
    block = first.shape[1]
    return jnp.concatenate([piece[pl.ds(b * block, block), :] for piece in (first, second) for b in range(2)], axis=1)


def prepare_kernel(
    mine_a, mine_b, got1, got2, got3, got4, factor, factor_other, diag_inv,
    far_high, far_low, turned_high, turned_low, own_part, products, partial,
):
    place, diagonal = own_place()
    beside, over, _ = places(place)
    block = mine_a.shape[1]

    def write(rows):
        far_high[...], far_low[...] = split(rows)
        turned_high[...], turned_low[...] = split(rows.T)

    @pl.when(diagonal)
    def _():
        write(factor_other[...])

    @pl.when(jnp.logical_not(diagonal))
    def _():
        write(factor[...])
        for j in range(own_part.shape[0]):
            inverse = split(diag_inv[j])
            own_part[j] = product(inverse, inverse, FIRST)
        rows = split(jnp.concatenate([row_of(mine_a, mine_b), row_of(got1, got4), row_of(got2, got3)], axis=0))
        products[...] = product(rows, (far_high[...], far_low[...]), PLAIN)
        factors = jnp.concatenate([factor_other[at(where, block), :] for where in (place, beside, over)], axis=0)
        partial[...] = product(rows, split(factors), FIRST)


def near_kernel(
    quadrant, got5, got6, most, own_high, own_low, factor_other, turned_high, turned_low, own_part, partial, cross
):
    place, diagonal = own_place()
    across = places(place)[2]
    width = cross.shape[1]

    @pl.when(diagonal)
    def _():
        own = own_high[...], own_low[...]
        partial[...] = product(split(quadrant[...]), own, PLAIN)
        value = split(partial[...])
        for j in range(cross.shape[0]):
            cross[j] = product(columns_of(own, j, width), columns_of(value, j, width), FIRST)

    @pl.when(jnp.logical_not(diagonal))
    def _():
        factors = split(factor_other[at(across, got5.shape[1]), :])
        partial[...] = most[...] + joined(split(row_of(got5, got6)), factors, FIRST)
        value = split(partial[...])
        for j in range(cross.shape[0]):
            rows = pl.ds(j * width, width)
            mixed = product((turned_high[rows, :], turned_low[rows, :]), columns_of(value, j, width), PLAIN)
            cross[j] = own_part[j] + (mixed + mixed.T)


def again_kernel(got, same):
    same[...] = got[...]


def joined(left, right, dims):
    (over,), (under,) = dims
    return lax.dot_general(
        jnp.concatenate([left[0], left[0], left[1]], axis=over),
        jnp.concatenate([right[0], right[1], right[0]], axis=under),
        (dims, ((), ())),
        preferred_element_type=jnp.float32,
    )


def early_parts(early, block):
    half = block // 2
    return [
        [
            early.at[pl.ds(start, size), pl.ds(n * block, block)]
            for start, size in ((0, block), (block, half), (block + half, half))
        ]
        + [early.at[pl.ds(n * SPARE, SPARE), pl.ds(3 * block, block)]]
        for n in range(3)
    ]


def far_kernel(got1, got2, got5, got7, early, far_high, far_low, turned_high, turned_low, cross, first, quadrant):
    place, diagonal = own_place()
    beside, over, across = places(place)
    width = cross.shape[1]

    @pl.when(diagonal)
    def _():
        symmetric(
            quadrant,
            ((parts(got1), place), (parts(got2), over), (parts(got5), beside), (parts(got7), across)),
        )
        value = split(product(split(quadrant[...]), (far_high[...], far_low[...]), PLAIN))
        for j in range(cross.shape[0]):
            rows = pl.ds(j * width, width)
            cross[j] = product((turned_high[rows, :], turned_low[rows, :]), columns_of(value, j, width), PLAIN)

    @pl.when(jnp.logical_not(diagonal))
    def _():
        quadrant[...] = jnp.zeros_like(quadrant)
        symmetric(quadrant, zip(early_parts(early, got1.shape[1]), (place, beside, over)))
        first[...] = product(split(quadrant[...]), (far_high[...], far_low[...]), PLAIN)


def panel_kernel(
    early_a, early_b, late, partial, far_high, far_low, turned_high, turned_low, near, near_other, far, first,
    sigma, diag, total, sigma_here, diag_here, sigma_sems, diag_sems,
):
    place, diagonal = own_place()
    beside, over, across = places(place)
    width = diag.shape[1]
    children = range(diag.shape[0])
    chunk = sigma.shape[0] // sigma_sems.shape[0]
    chunks = [pl.ds(c * chunk, chunk) for c in range(sigma_sems.shape[0])]

    def store(rows, c):
        return pltpu.make_async_copy(sigma_here.at[rows], sigma.at[rows], sigma_sems.at[c])

    diag_stores = [pltpu.make_async_copy(diag_here.at[j], diag.at[j], diag_sems.at[j]) for j in children]

    @pl.when(diagonal)
    def _():
        for j in children:
            diag_here[j] = (near[j] + near_other[j]) + far[j]
            diag_stores[j].start()
        early = [ref[pl.ds(c * chunk, chunk), :] for ref in (early_a, early_b) for c in range(ref.shape[0] // chunk)]
        for n, here in enumerate(early):
            rows = at((place, beside, over, across)[n], chunk)
            sigma_here[rows, :] = -(partial[rows, :] + here)
            store(rows, n).start()

    @pl.when(jnp.logical_not(diagonal))
    def _():
        block = late.shape[1]
        half = block // 2
        after, low = lax.rem(across + 1, 4), lax.rem(across, 2)
        piece_rows = pl.ds(pl.multiple_of(low * block + lax.div(across, 2) * half, half), half)

        def factors(rows):
            return far_high[rows, :], far_low[rows, :]

        following, opposite, top, ends = parts(late)
        own = split(unfolded(top[...], ends[pl.ds(0, 1), :]))
        following, opposite = split(following[...]), split(opposite[...])
        def finish(where, c, last):
            rows = at(where, block)
            sigma_here[rows, :] = -(partial[rows, :] + last)
            store(rows, c).start()
            total[rows, :] = last

        beyond, facing = lax.rem(across + 3, 4), lax.rem(across + 2, 4)
        finish(beyond, 0, first[at(beyond, block), :])
        here = factors(at(across, block))
        finish(after, 1, first[at(after, block), :] + joined(following, here, FIRST))
        rows = tuple(jnp.concatenate(pair, axis=1) for pair in zip(own, following))
        there = tuple(jnp.concatenate(pair, axis=0) for pair in zip(here, factors(at(after, block))))
        total[at(across, block), :] = first[at(across, block), :] + joined(rows, there, PLAIN)
        total[at(facing, block), :] = first[at(facing, block), :]
        total[piece_rows, :] += joined(opposite, factors(at(low + 2, block)), PLAIN)
        total[at(low + 2, block), :] += joined(opposite, factors(piece_rows), FIRST)
        finish(across, 2, total[at(across, block), :])
        finish(facing, 3, total[at(facing, block), :])
        value = split(total[...])
        for j in children:
            turned = pl.ds(j * width, width)
            inner = product((turned_high[turned, :], turned_low[turned, :]), columns_of(value, j, width), PLAIN)
            diag_here[j] = (near[j] + near_other[j]) + inner
            diag_stores[j].start()

    for copy in (*(store(rows, c) for c, rows in enumerate(chunks)), *diag_stores):
        copy.wait()


def call(kernel, out_shapes, flops, *args, specs=None, out_specs=None, scratch=()):
    moved = sum(a.size * a.dtype.itemsize for a in (*args, *out_shapes))
    return pl.pallas_call(
        kernel,
        out_shape=out_shapes,
        in_specs=specs or [VMEM] * len(args),
        out_specs=out_specs or [VMEM] * len(out_shapes),
        scratch_shapes=scratch,
        cost_estimate=pl.CostEstimate(flops=flops, bytes_accessed=moved, transcendentals=0),
        compiler_params=pltpu.CompilerParams(vmem_limit_bytes=32 * 1024 * 1024),
    )(*args)


def permute(value, mesh, diagonal_step, other_step=None):
    cfgs, prows, cores = (mesh.shape[axis] for axis in AXES)
    pairs = []
    for c in range(cfgs):
        for p in range(prows):
            for k in range(cores):
                step = diagonal_step if p // 4 == k else other_step
                to_cfg, to = (cfgs - 1 - c, p) if step is None else (c, p ^ step)
                pairs.append(((c * prows + p) * cores + k, (to_cfg * prows + to) * cores + (k ^ (p // 4) ^ (to // 4))))
    return lax.ppermute(value, AXES, pairs)


def exchange(value, mesh):
    cfgs, prows, cores = (mesh.shape[axis] for axis in AXES)
    return lax.ppermute(value, AXES, [(d, d ^ 1) for d in range(cfgs * prows * cores)])


def local_eight(mesh, sigma_top, panel_l, diag_inv, pattern):
    f32 = jnp.float32
    half_rows, own_columns = panel_l.shape
    block = sigma_top.shape[0]
    local_sn, width = diag_inv.shape[:2]
    shape = lambda *dims: jax.ShapeDtypeStruct(dims, f32)
    size = 2 * block + SPARE
    panel, square = shape(half_rows, own_columns), shape(half_rows, half_rows)
    children = shape(*diag_inv.shape)
    halves = [jax.ShapeDtypeStruct((half_rows, own_columns), jnp.bfloat16)] * 2
    turned = [jax.ShapeDtypeStruct((own_columns, half_rows), jnp.bfloat16)] * 2
    anywhere = pl.BlockSpec(memory_space=pl.ANY)
    in_hbm = lambda value: pltpu.with_memory_space_constraint(value, pltpu.HBM)
    step = 2 * half_rows * half_rows * own_columns
    mine_a, mine_b, mask = call(
        pieces_kernel,
        [shape(size, block)] * 2 + [shape(local_sn * (half_rows // block), width)],
        40 * step,
        in_hbm(sigma_top),
        in_hbm(pattern),
        specs=[anywhere] * 2,
        scratch=[
            pltpu.VMEM(sigma_top.shape, f32),
            pltpu.SMEM(pattern.shape, jnp.int32),
            pltpu.SemaphoreType.DMA((2,)),
        ],
    )
    got1 = permute(mine_a, mesh, 4, 1)
    got2 = permute(mine_a, mesh, 6, 2)
    got3 = permute(mine_b, mesh, 1, 2)
    got4 = permute(mine_b, mesh, 2, 1)
    got5 = permute(got1, mesh, 1, 2)
    got6 = permute(got4, mesh, 1, 2)
    (got2_again,) = call(again_kernel, [shape(size, block)], 40 * step, got2)
    got7 = permute(got2_again, mesh, 1)
    (got7_again,) = call(again_kernel, [shape(size, block)], 16 * step, got7)
    factor, *own_factor = call(
        factor_kernel,
        [panel, *halves],
        1,
        mask,
        panel_l,
        diag_inv,
    )
    factor_other = exchange(factor, mesh)
    *far_rows, own_part, products, most = call(
        prepare_kernel,
        [*halves, *turned, children, shape(3 * block, own_columns), panel],
        1,
        mine_a, mine_b, got1, got2, got3, got4, factor, factor_other, diag_inv,
    )
    own_half, sent_a, sent_b = call(
        own_half_kernel,
        [square] + [shape(half_rows // 2, own_columns)] * 2,
        36 * step,
        mine_a, got1, got2, got3, got4, got5, got6, products, *far_rows[:2],
    )
    early_a, early_b = exchange(sent_a, mesh), exchange(sent_b, mesh)
    partial, near = call(
        near_kernel,
        [panel, children],
        4 * step,
        own_half, got5, got6, most, *own_factor, factor_other, *far_rows[2:], own_part,
    )
    near_other = exchange(near, mesh)
    late = exchange(got7, mesh)
    far, first = call(
        far_kernel,
        [children, panel],
        1,
        got1, got2, got5, got7_again, early_a, *far_rows,
        scratch=[pltpu.VMEM(square.shape, f32)],
    )
    return tuple(
        call(
            panel_kernel,
            [panel, children],
            1,
            early_a, early_b, late, partial, *far_rows, near, near_other, far, first,
            out_specs=[anywhere] * 2,
            scratch=[
                pltpu.VMEM(square.shape, f32),
                pltpu.VMEM(panel.shape, f32),
                pltpu.VMEM(children.shape, f32),
                pltpu.SemaphoreType.DMA((half_rows // block,)),
                pltpu.SemaphoreType.DMA((local_sn,)),
            ],
        )
    )


def local_any(sigma_top, panel_l, diag_inv, pattern):
    half_rows = panel_l.shape[0]
    local_sn, width = diag_inv.shape[:2]
    row_mask = jnp.repeat(pattern.astype(jnp.float32), W // BLOCK_ROWS, axis=1)
    row_mask = lax.dynamic_slice_in_dim(row_mask, lax.axis_index("pcol") * half_rows, half_rows, 1)
    masked = panel_l.reshape(half_rows, local_sn, width) * jnp.transpose(row_mask)[:, :, None]
    factor = jnp.einsum("wns,nst->wnt", masked, diag_inv, precision=lax.Precision.HIGHEST)
    factor_flat = factor.reshape(half_rows, local_sn * width)
    whole = lax.all_gather(factor_flat, "pcol", axis=0, tiled=True)
    gathered = lax.all_gather(sigma_top, "prow", axis=0, tiled=True)
    sigma = -jnp.einsum("wv,wt->vt", gathered, whole, precision=lax.Precision.HIGHEST)
    sigma_three = sigma.reshape(half_rows, local_sn, width)
    cross = lax.psum(jnp.einsum("wnr,wnt->nrt", factor, sigma_three, precision=lax.Precision.HIGHEST), "pcol")
    own_part = jnp.einsum("nsr,nst->nrt", diag_inv, diag_inv, precision=lax.Precision.HIGHEST)
    return sigma, own_part - cross


def solution(mesh):
    in_specs = (
        P(("cfg", "prow"), "pcol"),
        P(("cfg", "pcol"), "prow"),
        P(("cfg", "prow"), None, None),
        P(("cfg", "prow"), None),
    )
    out_specs = (P(("cfg", "pcol"), "prow"), P(("cfg", "prow"), None, None))
    local = functools.partial(local_eight, mesh) if mesh.shape["prow"] == 8 else local_any
    return jax.shard_map(local, mesh=mesh, in_specs=in_specs, out_specs=out_specs, check_vma=False)
```

```python
import functools

import jax
import jax.numpy as jnp
from jax import lax
from jax.experimental import pallas as pl
from jax.experimental.pallas import tpu as pltpu
from jax.sharding import PartitionSpec as P

W = 1024
BLOCK_ROWS = 8
SPARE = 8
AXES = ("cfg", "prow", "pcol")
VMEM = pl.BlockSpec(memory_space=pltpu.VMEM)
SMEM = pl.BlockSpec(memory_space=pltpu.SMEM)


def split(value):
    high = value.astype(jnp.bfloat16)
    low = (value - high.astype(jnp.float32)).astype(jnp.bfloat16)
    return high, low


def product(left, right, dims):
    dot = functools.partial(lax.dot_general, dimension_numbers=(dims, ((), ())), preferred_element_type=jnp.float32)
    return dot(left[0], right[0]) + (dot(left[0], right[1]) + dot(left[1], right[0]))


PLAIN = ((1,), (0,))
FIRST = ((0,), (0,))


def factor_kernel(mask, panel, diag_inv, factor, own_high, own_low):
    children, width = diag_inv.shape[:2]
    here = mask.shape[0] // children
    block = panel.shape[0] // here
    for j in range(children):
        columns = pl.ds(j * width, width)
        masked = jnp.concatenate(
            [panel[pl.ds(r * block, block), columns] * mask[pl.ds(j * here + r, 1), :] for r in range(here)], axis=0
        )
        rows = product(split(masked), split(diag_inv[j]), PLAIN)
        factor[:, columns] = rows
        own_high[:, columns], own_low[:, columns] = split(rows)


def own_place():
    prow = lax.axis_index("prow")
    return lax.rem(prow, 4), lax.div(prow, 4) == lax.axis_index("pcol")


def places(place):
    beside = place + 1 - 2 * lax.rem(place, 2)
    return beside, lax.rem(place + 2, 4), lax.rem(beside + 2, 4)


def at(place, block):
    return pl.ds(pl.multiple_of(place * block, block), block)


def parts(piece):
    block = piece.shape[1]
    half, last = block // 2, 2 * block
    return [piece.at[pl.ds(start, size)] for start, size in ((0, block), (block, half), (block + half, half), (last, SPARE))]


def folded(block):
    half = block.shape[0] // 2
    top, bottom = block[:half], block[half:]
    row, lane = (lax.broadcasted_iota(jnp.int32, top.shape, axis) for axis in (0, 1))
    top = jnp.where((lane < half) & (row > lane), pltpu.roll(bottom, half, 1), top)
    return top, jnp.sum(jnp.where(row == lane - half, bottom, 0.0), axis=0, keepdims=True)


def unfolded(top, ends):
    half = top.shape[0]
    row, lane = (lax.broadcasted_iota(jnp.int32, top.shape, axis) for axis in (0, 1))
    turned = jnp.concatenate([top, jnp.zeros_like(top)], axis=0).T
    upper = jnp.where((lane < half) & (row > lane), turned[:half], top)
    own = jnp.where(row < lane - half, pltpu.roll(turned[:half], half, 1), ends)
    own = jnp.where(row > lane - half, pltpu.roll(top, half, 1), own)
    return jnp.concatenate([upper, jnp.where(lane < half, turned[half:], own)], axis=0)


def pieces_kernel(sigma_top, pattern, first, second, mask, own, pattern_here, sems):
    place, diagonal = own_place()
    loads = [
        pltpu.make_async_copy(source, here, sems.at[n])
        for n, (source, here) in enumerate(
            ((sigma_top, own), (pattern, pattern_here))
        )
    ]
    for load in loads:
        load.start()
    loads[0].wait()
    block = own.shape[0]
    half = block // 2

    @pl.when(diagonal)
    def _():
        opposite = at(lax.rem(place + 2, 4), block)
        top, ends = folded(own[:, at(place, block)])
        for piece in (first, second):
            following, _, folded_top, folded_ends = parts(piece)
            following[...] = own[:, at(lax.rem(place + 1, 4), block)]
            folded_top[...] = top
            folded_ends[...] = jnp.broadcast_to(ends, folded_ends.shape)

        @pl.when(place < 2)
        def _():
            for piece in (first, second):
                parts(piece)[1][...] = own[pl.ds(0, half), opposite]

        @pl.when(place >= 2)
        def _():
            turned = own[:, opposite].T
            for piece in (first, second):
                parts(piece)[1][...] = turned[half:]

    @pl.when(jnp.logical_not(diagonal))
    def _():
        for n, piece in enumerate((first, second)):
            for b in range(2):
                piece[pl.ds(b * block, block), :] = own[:, pl.ds((2 * n + b) * block, block)]
            piece[pl.ds(2 * block, SPARE), :] = jnp.zeros((SPARE, block), jnp.float32)

    loads[1].wait()
    core = lax.axis_index("pcol")
    here = mask.shape[0] // pattern.shape[0]
    for j in range(pattern.shape[0]):
        for r in range(here):
            kept = pattern_here[j, core * here + r].astype(jnp.float32)
            mask[pl.ds(j * here + r, 1), :] = jnp.full((1, mask.shape[1]), kept, jnp.float32)


def symmetric(quadrant, pieces):
    block = quadrant.shape[0] // 4
    half = block // 2
    for piece, place in pieces:
        rows = at(place, block)
        following, opposite, top, ends = piece
        quadrant[rows, at(place, block)] = unfolded(top[...], ends[pl.ds(0, 1), :])
        quadrant[rows, at(lax.rem(place + 1, 4), block)] = following[...]
        low = lax.rem(place, 2)
        quadrant[
            pl.ds(pl.multiple_of(low * block + lax.div(place, 2) * half, half), half), at(low + 2, block)
        ] = opposite[...]
    for row, column in ((0, 1), (1, 2), (2, 3), (3, 0), (0, 2), (1, 3)):
        rows, columns = pl.ds(row * block, block), pl.ds(column * block, block)
        quadrant[columns, rows] = quadrant[rows, columns].T


def row_blocks(quadrant, where, halves):
    block = quadrant.shape[0] // 4
    for n, piece in enumerate(halves):
        for b in range(2):
            quadrant[at(where, block), pl.ds((2 * n + b) * block, block)] = piece[pl.ds(b * block, block), :]


def own_half_kernel(mine_a, got1, got2, got3, got4, got5, got6, products, far_high, far_low, quadrant, sent_a, sent_b):
    place, diagonal = own_place()
    beside, over, across = places(place)
    rows, block = sent_a.shape[0], quadrant.shape[0] // 4

    @pl.when(diagonal)
    def _():
        symmetric(
            quadrant,
            ((parts(mine_a), place), (parts(got3), beside), (parts(got4), over), (parts(got6), across)),
        )
        for n, piece in enumerate((got1, got5, got2)):
            rest = piece.shape[0] - rows
            sent_a[:, pl.ds(n * block, block)] = piece[pl.ds(0, rows), :]
            sent_a[pl.ds(n * rest, rest), pl.ds(3 * block, block)] = piece[pl.ds(rows, rest), :]

    @pl.when(jnp.logical_not(diagonal))
    def _():
        last = joined(split(row_of(got5, got6)), (far_high[...], far_low[...]), PLAIN)
        sent_a[...] = products[pl.ds(0, rows), :]
        sent_b[pl.ds(0, block), :] = products[pl.ds(rows, block), :]
        sent_b[pl.ds(block, block), :] = last


def columns_of(value, j, width):
    return tuple(part[:, j * width : (j + 1) * width] for part in value)


def row_of(first, second):
    block = first.shape[1]
    return jnp.concatenate([piece[pl.ds(b * block, block), :] for piece in (first, second) for b in range(2)], axis=1)


def prepare_kernel(
    mine_a, mine_b, got1, got2, got3, got4, factor, factor_other, diag_inv,
    far_high, far_low, turned_high, turned_low, own_part, products, partial,
):
    place, diagonal = own_place()
    beside, over, _ = places(place)
    block = mine_a.shape[1]

    def write(rows):
        far_high[...], far_low[...] = split(rows)
        turned_high[...], turned_low[...] = split(rows.T)

    @pl.when(diagonal)
    def _():
        write(factor_other[...])

    @pl.when(jnp.logical_not(diagonal))
    def _():
        write(factor[...])
        for j in range(own_part.shape[0]):
            inverse = split(diag_inv[j])
            own_part[j] = product(inverse, inverse, FIRST)
        rows = split(jnp.concatenate([row_of(mine_a, mine_b), row_of(got1, got4), row_of(got2, got3)], axis=0))
        products[...] = product(rows, (far_high[...], far_low[...]), PLAIN)
        factors = jnp.concatenate([factor_other[at(where, block), :] for where in (place, beside, over)], axis=0)
        partial[...] = product(rows, split(factors), FIRST)


def near_kernel(
    quadrant, got5, got6, most, own_high, own_low, factor_other, turned_high, turned_low, own_part, partial, cross
):
    place, diagonal = own_place()
    across = places(place)[2]
    width = cross.shape[1]

    @pl.when(diagonal)
    def _():
        own = own_high[...], own_low[...]
        partial[...] = product(split(quadrant[...]), own, PLAIN)
        value = split(partial[...])
        for j in range(cross.shape[0]):
            cross[j] = product(columns_of(own, j, width), columns_of(value, j, width), FIRST)

    @pl.when(jnp.logical_not(diagonal))
    def _():
        factors = split(factor_other[at(across, got5.shape[1]), :])
        partial[...] = most[...] + joined(split(row_of(got5, got6)), factors, FIRST)
        value = split(partial[...])
        for j in range(cross.shape[0]):
            rows = pl.ds(j * width, width)
            mixed = product((turned_high[rows, :], turned_low[rows, :]), columns_of(value, j, width), PLAIN)
            cross[j] = own_part[j] + (mixed + mixed.T)


def again_kernel(got, same):
    same[...] = got[...]


def joined(left, right, dims):
    (over,), (under,) = dims
    return lax.dot_general(
        jnp.concatenate([left[0], left[0], left[1]], axis=over),
        jnp.concatenate([right[0], right[1], right[0]], axis=under),
        (dims, ((), ())),
        preferred_element_type=jnp.float32,
    )


def early_parts(early, block):
    half = block // 2
    return [
        [
            early.at[pl.ds(start, size), pl.ds(n * block, block)]
            for start, size in ((0, block), (block, half), (block + half, half))
        ]
        + [early.at[pl.ds(n * SPARE, SPARE), pl.ds(3 * block, block)]]
        for n in range(3)
    ]


def far_kernel(got1, got2, got5, got7, early, far_high, far_low, turned_high, turned_low, cross, first, quadrant):
    place, diagonal = own_place()
    beside, over, across = places(place)
    width = cross.shape[1]

    @pl.when(diagonal)
    def _():
        symmetric(
            quadrant,
            ((parts(got1), place), (parts(got2), over), (parts(got5), beside), (parts(got7), across)),
        )
        value = split(product(split(quadrant[...]), (far_high[...], far_low[...]), PLAIN))
        for j in range(cross.shape[0]):
            rows = pl.ds(j * width, width)
            cross[j] = product((turned_high[rows, :], turned_low[rows, :]), columns_of(value, j, width), PLAIN)

    @pl.when(jnp.logical_not(diagonal))
    def _():
        block = got1.shape[1]
        half, low = block // 2, lax.rem(across, 2)
        nothing = jnp.zeros((block, block), jnp.float32)
        quadrant[at(across, block), at(across, block)] = nothing
        quadrant[at(across, block), at(lax.rem(across + 1, 4), block)] = nothing
        quadrant[
            pl.ds(pl.multiple_of(low * block + lax.div(across, 2) * half, half), half), at(low + 2, block)
        ] = nothing[:half]
        symmetric(quadrant, zip(early_parts(early, got1.shape[1]), (place, beside, over)))
        first[...] = product(split(quadrant[...]), (far_high[...], far_low[...]), PLAIN)


def panel_kernel(
    early_a, early_b, late, partial, far_high, far_low, turned_high, turned_low, near, near_other, far, first,
    sigma, diag, total, sigma_here, diag_here, sigma_sems, diag_sems,
):
    place, diagonal = own_place()
    beside, over, across = places(place)
    width = diag.shape[1]
    children = range(diag.shape[0])
    chunk = sigma.shape[0] // sigma_sems.shape[0]
    chunks = [pl.ds(c * chunk, chunk) for c in range(sigma_sems.shape[0])]

    def store(rows, c):
        return pltpu.make_async_copy(sigma_here.at[rows], sigma.at[rows], sigma_sems.at[c])

    diag_stores = [pltpu.make_async_copy(diag_here.at[j], diag.at[j], diag_sems.at[j]) for j in children]

    @pl.when(diagonal)
    def _():
        for j in children:
            diag_here[j] = (near[j] + near_other[j]) + far[j]
            diag_stores[j].start()
        early = [ref[pl.ds(c * chunk, chunk), :] for ref in (early_a, early_b) for c in range(ref.shape[0] // chunk)]
        for n, here in enumerate(early):
            rows = at((place, beside, over, across)[n], chunk)
            sigma_here[rows, :] = -(partial[rows, :] + here)
            store(rows, n).start()

    @pl.when(jnp.logical_not(diagonal))
    def _():
        block = late.shape[1]
        half = block // 2
        after, low = lax.rem(across + 1, 4), lax.rem(across, 2)
        piece_rows = pl.ds(pl.multiple_of(low * block + lax.div(across, 2) * half, half), half)

        def factors(rows):
            return far_high[rows, :], far_low[rows, :]

        following, opposite, top, ends = parts(late)
        own = split(unfolded(top[...], ends[pl.ds(0, 1), :]))
        following, opposite = split(following[...]), split(opposite[...])
        def finish(where, c, last):
            rows = at(where, block)
            sigma_here[rows, :] = -(partial[rows, :] + last)
            store(rows, c).start()
            total[rows, :] = last

        beyond, facing = lax.rem(across + 3, 4), lax.rem(across + 2, 4)
        finish(beyond, 0, first[at(beyond, block), :])
        here = factors(at(across, block))
        finish(after, 1, first[at(after, block), :] + joined(following, here, FIRST))
        rows = tuple(jnp.concatenate(pair, axis=1) for pair in zip(own, following))
        there = tuple(jnp.concatenate(pair, axis=0) for pair in zip(here, factors(at(after, block))))
        total[at(across, block), :] = first[at(across, block), :] + joined(rows, there, PLAIN)
        total[at(facing, block), :] = first[at(facing, block), :]
        total[piece_rows, :] += joined(opposite, factors(at(low + 2, block)), PLAIN)
        total[at(low + 2, block), :] += joined(opposite, factors(piece_rows), FIRST)
        finish(across, 2, total[at(across, block), :])
        finish(facing, 3, total[at(facing, block), :])
        value = split(total[...])
        for j in children:
            turned = pl.ds(j * width, width)
            inner = product((turned_high[turned, :], turned_low[turned, :]), columns_of(value, j, width), PLAIN)
            diag_here[j] = (near[j] + near_other[j]) + inner
            diag_stores[j].start()

    for copy in (*(store(rows, c) for c, rows in enumerate(chunks)), *diag_stores):
        copy.wait()


def call(kernel, out_shapes, flops, *args, specs=None, out_specs=None, scratch=()):
    moved = sum(a.size * a.dtype.itemsize for a in (*args, *out_shapes))
    return pl.pallas_call(
        kernel,
        out_shape=out_shapes,
        in_specs=specs or [VMEM] * len(args),
        out_specs=out_specs or [VMEM] * len(out_shapes),
        scratch_shapes=scratch,
        cost_estimate=pl.CostEstimate(flops=flops, bytes_accessed=moved, transcendentals=0),
        compiler_params=pltpu.CompilerParams(vmem_limit_bytes=32 * 1024 * 1024),
    )(*args)


def permute(value, mesh, diagonal_step, other_step=None):
    cfgs, prows, cores = (mesh.shape[axis] for axis in AXES)
    pairs = []
    for c in range(cfgs):
        for p in range(prows):
            for k in range(cores):
                step = diagonal_step if p // 4 == k else other_step
                to_cfg, to = (cfgs - 1 - c, p) if step is None else (c, p ^ step)
                pairs.append(((c * prows + p) * cores + k, (to_cfg * prows + to) * cores + (k ^ (p // 4) ^ (to // 4))))
    return lax.ppermute(value, AXES, pairs)


def exchange(value, mesh):
    cfgs, prows, cores = (mesh.shape[axis] for axis in AXES)
    return lax.ppermute(value, AXES, [(d, d ^ 1) for d in range(cfgs * prows * cores)])


def local_eight(mesh, sigma_top, panel_l, diag_inv, pattern):
    f32 = jnp.float32
    half_rows, own_columns = panel_l.shape
    block = sigma_top.shape[0]
    local_sn, width = diag_inv.shape[:2]
    shape = lambda *dims: jax.ShapeDtypeStruct(dims, f32)
    size = 2 * block + SPARE
    panel, square = shape(half_rows, own_columns), shape(half_rows, half_rows)
    children = shape(*diag_inv.shape)
    halves = [jax.ShapeDtypeStruct((half_rows, own_columns), jnp.bfloat16)] * 2
    turned = [jax.ShapeDtypeStruct((own_columns, half_rows), jnp.bfloat16)] * 2
    anywhere = pl.BlockSpec(memory_space=pl.ANY)
    in_hbm = lambda value: pltpu.with_memory_space_constraint(value, pltpu.HBM)
    step = 2 * half_rows * half_rows * own_columns
    mine_a, mine_b, mask = call(
        pieces_kernel,
        [shape(size, block)] * 2 + [shape(local_sn * (half_rows // block), width)],
        40 * step,
        in_hbm(sigma_top),
        in_hbm(pattern),
        specs=[anywhere] * 2,
        scratch=[
            pltpu.VMEM(sigma_top.shape, f32),
            pltpu.SMEM(pattern.shape, jnp.int32),
            pltpu.SemaphoreType.DMA((2,)),
        ],
    )
    got1 = permute(mine_a, mesh, 4, 1)
    got2 = permute(mine_a, mesh, 6, 2)
    got3 = permute(mine_b, mesh, 1, 2)
    got4 = permute(mine_b, mesh, 2, 1)
    got5 = permute(got1, mesh, 1, 2)
    got6 = permute(got4, mesh, 1, 2)
    (got2_again,) = call(again_kernel, [shape(size, block)], 40 * step, got2)
    got7 = permute(got2_again, mesh, 1)
    (got7_again,) = call(again_kernel, [shape(size, block)], 16 * step, got7)
    factor, *own_factor = call(
        factor_kernel,
        [panel, *halves],
        1,
        mask,
        panel_l,
        diag_inv,
    )
    factor_other = exchange(factor, mesh)
    *far_rows, own_part, products, most = call(
        prepare_kernel,
        [*halves, *turned, children, shape(3 * block, own_columns), panel],
        1,
        mine_a, mine_b, got1, got2, got3, got4, factor, factor_other, diag_inv,
    )
    own_half, sent_a, sent_b = call(
        own_half_kernel,
        [square] + [shape(half_rows // 2, own_columns)] * 2,
        36 * step,
        mine_a, got1, got2, got3, got4, got5, got6, products, *far_rows[:2],
    )
    early_a, early_b = exchange(sent_a, mesh), exchange(sent_b, mesh)
    partial, near = call(
        near_kernel,
        [panel, children],
        4 * step,
        own_half, got5, got6, most, *own_factor, factor_other, *far_rows[2:], own_part,
    )
    near_other = exchange(near, mesh)
    late = exchange(got7, mesh)
    far, first = call(
        far_kernel,
        [children, panel],
        1,
        got1, got2, got5, got7_again, early_a, *far_rows,
        scratch=[pltpu.VMEM(square.shape, f32)],
    )
    return tuple(
        call(
            panel_kernel,
            [panel, children],
            1,
            early_a, early_b, late, partial, *far_rows, near, near_other, far, first,
            out_specs=[anywhere] * 2,
            scratch=[
                pltpu.VMEM(square.shape, f32),
                pltpu.VMEM(panel.shape, f32),
                pltpu.VMEM(children.shape, f32),
                pltpu.SemaphoreType.DMA((half_rows // block,)),
                pltpu.SemaphoreType.DMA((local_sn,)),
            ],
        )
    )


def local_any(sigma_top, panel_l, diag_inv, pattern):
    half_rows = panel_l.shape[0]
    local_sn, width = diag_inv.shape[:2]
    row_mask = jnp.repeat(pattern.astype(jnp.float32), W // BLOCK_ROWS, axis=1)
    row_mask = lax.dynamic_slice_in_dim(row_mask, lax.axis_index("pcol") * half_rows, half_rows, 1)
    masked = panel_l.reshape(half_rows, local_sn, width) * jnp.transpose(row_mask)[:, :, None]
    factor = jnp.einsum("wns,nst->wnt", masked, diag_inv, precision=lax.Precision.HIGHEST)
    factor_flat = factor.reshape(half_rows, local_sn * width)
    whole = lax.all_gather(factor_flat, "pcol", axis=0, tiled=True)
    gathered = lax.all_gather(sigma_top, "prow", axis=0, tiled=True)
    sigma = -jnp.einsum("wv,wt->vt", gathered, whole, precision=lax.Precision.HIGHEST)
    sigma_three = sigma.reshape(half_rows, local_sn, width)
    cross = lax.psum(jnp.einsum("wnr,wnt->nrt", factor, sigma_three, precision=lax.Precision.HIGHEST), "pcol")
    own_part = jnp.einsum("nsr,nst->nrt", diag_inv, diag_inv, precision=lax.Precision.HIGHEST)
    return sigma, own_part - cross


def solution(mesh):
    in_specs = (
        P(("cfg", "prow"), "pcol"),
        P(("cfg", "pcol"), "prow"),
        P(("cfg", "prow"), None, None),
        P(("cfg", "prow"), None),
    )
    out_specs = (P(("cfg", "pcol"), "prow"), P(("cfg", "prow"), None, None))
    local = functools.partial(local_eight, mesh) if mesh.shape["prow"] == 8 else local_any
    return jax.shard_map(local, mesh=mesh, in_specs=in_specs, out_specs=out_specs, check_vma=False)
```

```python
import functools

import jax
import jax.numpy as jnp
from jax import lax
from jax.experimental import pallas as pl
from jax.experimental.pallas import tpu as pltpu
from jax.sharding import PartitionSpec as P

W = 1024
BLOCK_ROWS = 8
SPARE = 8
AXES = ("cfg", "prow", "pcol")
VMEM = pl.BlockSpec(memory_space=pltpu.VMEM)
SMEM = pl.BlockSpec(memory_space=pltpu.SMEM)


def split(value):
    high = value.astype(jnp.bfloat16)
    low = (value - high.astype(jnp.float32)).astype(jnp.bfloat16)
    return high, low


def product(left, right, dims):
    dot = functools.partial(lax.dot_general, dimension_numbers=(dims, ((), ())), preferred_element_type=jnp.float32)
    return dot(left[0], right[0]) + (dot(left[0], right[1]) + dot(left[1], right[0]))


PLAIN = ((1,), (0,))
FIRST = ((0,), (0,))


def factor_kernel(mask, panel, diag_inv, factor, own_high, own_low):
    children, width = diag_inv.shape[:2]
    here = mask.shape[0] // children
    block = panel.shape[0] // here
    for j in range(children):
        columns = pl.ds(j * width, width)
        masked = jnp.concatenate(
            [panel[pl.ds(r * block, block), columns] * mask[pl.ds(j * here + r, 1), :] for r in range(here)], axis=0
        )
        rows = product(split(masked), split(diag_inv[j]), PLAIN)
        factor[:, columns] = rows
        own_high[:, columns], own_low[:, columns] = split(rows)


def own_place():
    prow = lax.axis_index("prow")
    return lax.rem(prow, 4), lax.div(prow, 4) == lax.axis_index("pcol")


def places(place):
    beside = place + 1 - 2 * lax.rem(place, 2)
    return beside, lax.rem(place + 2, 4), lax.rem(beside + 2, 4)


def at(place, block):
    return pl.ds(pl.multiple_of(place * block, block), block)


def parts(piece):
    block = piece.shape[1]
    half, last = block // 2, 2 * block
    return [piece.at[pl.ds(start, size)] for start, size in ((0, block), (block, half), (block + half, half), (last, SPARE))]


def folded(block):
    half = block.shape[0] // 2
    top, bottom = block[:half], block[half:]
    row, lane = (lax.broadcasted_iota(jnp.int32, top.shape, axis) for axis in (0, 1))
    top = jnp.where((lane < half) & (row > lane), pltpu.roll(bottom, half, 1), top)
    return top, jnp.sum(jnp.where(row == lane - half, bottom, 0.0), axis=0, keepdims=True)


def unfolded(top, ends):
    half = top.shape[0]
    row, lane = (lax.broadcasted_iota(jnp.int32, top.shape, axis) for axis in (0, 1))
    turned = jnp.concatenate([top, jnp.zeros_like(top)], axis=0).T
    upper = jnp.where((lane < half) & (row > lane), turned[:half], top)
    own = jnp.where(row < lane - half, pltpu.roll(turned[:half], half, 1), ends)
    own = jnp.where(row > lane - half, pltpu.roll(top, half, 1), own)
    return jnp.concatenate([upper, jnp.where(lane < half, turned[half:], own)], axis=0)


def pieces_kernel(sigma_top, pattern, first, second, mask, own, pattern_here, sems):
    place, diagonal = own_place()
    loads = [
        pltpu.make_async_copy(source, here, sems.at[n])
        for n, (source, here) in enumerate(
            ((sigma_top, own), (pattern, pattern_here))
        )
    ]
    for load in loads:
        load.start()
    loads[0].wait()
    block = own.shape[0]
    half = block // 2

    @pl.when(diagonal)
    def _():
        opposite = at(lax.rem(place + 2, 4), block)
        top, ends = folded(own[:, at(place, block)])
        for piece in (first, second):
            following, _, folded_top, folded_ends = parts(piece)
            following[...] = own[:, at(lax.rem(place + 1, 4), block)]
            folded_top[...] = top
            folded_ends[...] = jnp.broadcast_to(ends, folded_ends.shape)

        @pl.when(place < 2)
        def _():
            for piece in (first, second):
                parts(piece)[1][...] = own[pl.ds(0, half), opposite]

        @pl.when(place >= 2)
        def _():
            turned = own[:, opposite].T
            for piece in (first, second):
                parts(piece)[1][...] = turned[half:]

    @pl.when(jnp.logical_not(diagonal))
    def _():
        for n, piece in enumerate((first, second)):
            for b in range(2):
                piece[pl.ds(b * block, block), :] = own[:, pl.ds((2 * n + b) * block, block)]
            piece[pl.ds(2 * block, SPARE), :] = jnp.zeros((SPARE, block), jnp.float32)

    loads[1].wait()
    core = lax.axis_index("pcol")
    here = mask.shape[0] // pattern.shape[0]
    for j in range(pattern.shape[0]):
        for r in range(here):
            kept = pattern_here[j, core * here + r].astype(jnp.float32)
            mask[pl.ds(j * here + r, 1), :] = jnp.full((1, mask.shape[1]), kept, jnp.float32)


def symmetric(quadrant, pieces):
    block = quadrant.shape[0] // 4
    half = block // 2
    for piece, place in pieces:
        rows = at(place, block)
        following, opposite, top, ends = piece
        quadrant[rows, at(place, block)] = unfolded(top[...], ends[pl.ds(0, 1), :])
        quadrant[rows, at(lax.rem(place + 1, 4), block)] = following[...]
        low = lax.rem(place, 2)
        quadrant[
            pl.ds(pl.multiple_of(low * block + lax.div(place, 2) * half, half), half), at(low + 2, block)
        ] = opposite[...]
    for row, column in ((0, 1), (1, 2), (2, 3), (3, 0), (0, 2), (1, 3)):
        rows, columns = pl.ds(row * block, block), pl.ds(column * block, block)
        quadrant[columns, rows] = quadrant[rows, columns].T


def row_blocks(quadrant, where, halves):
    block = quadrant.shape[0] // 4
    for n, piece in enumerate(halves):
        for b in range(2):
            quadrant[at(where, block), pl.ds((2 * n + b) * block, block)] = piece[pl.ds(b * block, block), :]


def own_half_kernel(mine_a, got1, got2, got3, got4, got5, got6, products, far_high, far_low, quadrant, sent_a, sent_b):
    place, diagonal = own_place()
    beside, over, across = places(place)
    rows, block = sent_a.shape[0], quadrant.shape[0] // 4

    @pl.when(diagonal)
    def _():
        symmetric(
            quadrant,
            ((parts(mine_a), place), (parts(got3), beside), (parts(got4), over), (parts(got6), across)),
        )
        for n, piece in enumerate((got1, got5, got2)):
            rest = piece.shape[0] - rows
            sent_a[:, pl.ds(n * block, block)] = piece[pl.ds(0, rows), :]
            sent_a[pl.ds(n * rest, rest), pl.ds(3 * block, block)] = piece[pl.ds(rows, rest), :]

    @pl.when(jnp.logical_not(diagonal))
    def _():
        last = joined(split(row_of(got5, got6)), (far_high[...], far_low[...]), PLAIN)
        sent_a[...] = products[pl.ds(0, rows), :]
        sent_b[pl.ds(0, block), :] = products[pl.ds(rows, block), :]
        sent_b[pl.ds(block, block), :] = last


def columns_of(value, j, width):
    return tuple(part[:, j * width : (j + 1) * width] for part in value)


def row_of(first, second):
    block = first.shape[1]
    return jnp.concatenate([piece[pl.ds(b * block, block), :] for piece in (first, second) for b in range(2)], axis=1)


def prepare_kernel(
    mine_a, mine_b, got1, got2, got3, got4, factor, factor_other, diag_inv,
    far_high, far_low, turned_high, turned_low, own_part, products, partial,
):
    place, diagonal = own_place()
    beside, over, _ = places(place)
    block = mine_a.shape[1]

    def write(rows):
        far_high[...], far_low[...] = split(rows)
        turned_high[...], turned_low[...] = split(rows.T)

    @pl.when(diagonal)
    def _():
        write(factor_other[...])

    @pl.when(jnp.logical_not(diagonal))
    def _():
        write(factor[...])
        for j in range(own_part.shape[0]):
            inverse = split(diag_inv[j])
            own_part[j] = product(inverse, inverse, FIRST)
        rows = split(jnp.concatenate([row_of(mine_a, mine_b), row_of(got1, got4), row_of(got2, got3)], axis=0))
        products[...] = product(rows, (far_high[...], far_low[...]), PLAIN)
        factors = jnp.concatenate([factor_other[at(where, block), :] for where in (place, beside, over)], axis=0)
        partial[...] = product(rows, split(factors), FIRST)


def near_kernel(
    quadrant, got5, got6, most, own_high, own_low, factor_other, turned_high, turned_low, own_part, partial, cross
):
    place, diagonal = own_place()
    across = places(place)[2]
    width = cross.shape[1]

    @pl.when(diagonal)
    def _():
        own = own_high[...], own_low[...]
        partial[...] = product(split(quadrant[...]), own, PLAIN)
        value = split(partial[...])
        for j in range(cross.shape[0]):
            cross[j] = product(columns_of(own, j, width), columns_of(value, j, width), FIRST)

    @pl.when(jnp.logical_not(diagonal))
    def _():
        factors = split(factor_other[at(across, got5.shape[1]), :])
        partial[...] = most[...] + joined(split(row_of(got5, got6)), factors, FIRST)
        value = split(partial[...])
        for j in range(cross.shape[0]):
            rows = pl.ds(j * width, width)
            mixed = product((turned_high[rows, :], turned_low[rows, :]), columns_of(value, j, width), PLAIN)
            cross[j] = own_part[j] + (mixed + mixed.T)


def again_kernel(got, same):
    same[...] = got[...]


def joined(left, right, dims):
    (over,), (under,) = dims
    return lax.dot_general(
        jnp.concatenate([left[0], left[0], left[1]], axis=over),
        jnp.concatenate([right[0], right[1], right[0]], axis=under),
        (dims, ((), ())),
        preferred_element_type=jnp.float32,
    )


def early_parts(early, block):
    half = block // 2
    return [
        [
            early.at[pl.ds(start, size), pl.ds(n * block, block)]
            for start, size in ((0, block), (block, half), (block + half, half))
        ]
        + [early.at[pl.ds(n * SPARE, SPARE), pl.ds(3 * block, block)]]
        for n in range(3)
    ]


def far_kernel(got1, got2, got5, got7, early, far_high, far_low, turned_high, turned_low, cross, first, quadrant):
    place, diagonal = own_place()
    beside, over, across = places(place)
    width = cross.shape[1]

    @pl.when(diagonal)
    def _():
        symmetric(
            quadrant,
            ((parts(got1), place), (parts(got2), over), (parts(got5), beside), (parts(got7), across)),
        )
        value = split(product(split(quadrant[...]), (far_high[...], far_low[...]), PLAIN))
        for j in range(cross.shape[0]):
            rows = pl.ds(j * width, width)
            cross[j] = product((turned_high[rows, :], turned_low[rows, :]), columns_of(value, j, width), PLAIN)

    @pl.when(jnp.logical_not(diagonal))
    def _():
        quadrant[...] = jnp.zeros_like(quadrant)
        symmetric(quadrant, zip(early_parts(early, got1.shape[1]), (place, beside, over)))
        first[...] = product(split(quadrant[...]), (far_high[...], far_low[...]), PLAIN)


def panel_kernel(
    early_a, early_b, late, partial, far_high, far_low, turned_high, turned_low, near, near_other, far, first,
    sigma, diag, total, sigma_here, diag_here, sigma_sems, diag_sems,
):
    place, diagonal = own_place()
    beside, over, across = places(place)
    width = diag.shape[1]
    children = range(diag.shape[0])
    chunk = sigma.shape[0] // sigma_sems.shape[0]
    chunks = [pl.ds(c * chunk, chunk) for c in range(sigma_sems.shape[0])]

    def store(rows, c):
        return pltpu.make_async_copy(sigma_here.at[rows], sigma.at[rows], sigma_sems.at[c])

    diag_stores = [pltpu.make_async_copy(diag_here.at[j], diag.at[j], diag_sems.at[j]) for j in children]

    @pl.when(diagonal)
    def _():
        early = [ref[pl.ds(c * chunk, chunk), :] for ref in (early_a, early_b) for c in range(ref.shape[0] // chunk)]
        for n, here in enumerate(early):
            rows = at((place, beside, over, across)[n], chunk)
            sigma_here[rows, :] = -(partial[rows, :] + here)
            store(rows, n).start()
        for j in children:
            diag_here[j] = (near[j] + near_other[j]) + far[j]
            diag_stores[j].start()

    @pl.when(jnp.logical_not(diagonal))
    def _():
        block = late.shape[1]
        half = block // 2
        after, low = lax.rem(across + 1, 4), lax.rem(across, 2)
        piece_rows = pl.ds(pl.multiple_of(low * block + lax.div(across, 2) * half, half), half)

        def factors(rows):
            return far_high[rows, :], far_low[rows, :]

        following, opposite, top, ends = parts(late)
        own = split(unfolded(top[...], ends[pl.ds(0, 1), :]))
        following, opposite = split(following[...]), split(opposite[...])
        def finish(where, c, last):
            rows = at(where, block)
            sigma_here[rows, :] = -(partial[rows, :] + last)
            store(rows, c).start()
            total[rows, :] = last

        beyond, facing = lax.rem(across + 3, 4), lax.rem(across + 2, 4)
        finish(beyond, 0, first[at(beyond, block), :])
        here = factors(at(across, block))
        finish(after, 1, first[at(after, block), :] + joined(following, here, FIRST))
        rows = tuple(jnp.concatenate(pair, axis=1) for pair in zip(own, following))
        there = tuple(jnp.concatenate(pair, axis=0) for pair in zip(here, factors(at(after, block))))
        total[at(across, block), :] = first[at(across, block), :] + joined(rows, there, PLAIN)
        total[at(facing, block), :] = first[at(facing, block), :]
        total[piece_rows, :] += joined(opposite, factors(at(low + 2, block)), PLAIN)
        total[at(low + 2, block), :] += joined(opposite, factors(piece_rows), FIRST)
        finish(across, 2, total[at(across, block), :])
        finish(facing, 3, total[at(facing, block), :])
        value = split(total[...])
        for j in children:
            turned = pl.ds(j * width, width)
            inner = product((turned_high[turned, :], turned_low[turned, :]), columns_of(value, j, width), PLAIN)
            diag_here[j] = (near[j] + near_other[j]) + inner
            diag_stores[j].start()

    for copy in (*(store(rows, c) for c, rows in enumerate(chunks)), *diag_stores):
        copy.wait()


def call(kernel, out_shapes, flops, *args, specs=None, out_specs=None, scratch=()):
    moved = sum(a.size * a.dtype.itemsize for a in (*args, *out_shapes))
    return pl.pallas_call(
        kernel,
        out_shape=out_shapes,
        in_specs=specs or [VMEM] * len(args),
        out_specs=out_specs or [VMEM] * len(out_shapes),
        scratch_shapes=scratch,
        cost_estimate=pl.CostEstimate(flops=flops, bytes_accessed=moved, transcendentals=0),
        compiler_params=pltpu.CompilerParams(vmem_limit_bytes=32 * 1024 * 1024),
    )(*args)


def permute(value, mesh, diagonal_step, other_step=None):
    cfgs, prows, cores = (mesh.shape[axis] for axis in AXES)
    pairs = []
    for c in range(cfgs):
        for p in range(prows):
            for k in range(cores):
                step = diagonal_step if p // 4 == k else other_step
                to_cfg, to = (cfgs - 1 - c, p) if step is None else (c, p ^ step)
                pairs.append(((c * prows + p) * cores + k, (to_cfg * prows + to) * cores + (k ^ (p // 4) ^ (to // 4))))
    return lax.ppermute(value, AXES, pairs)


def exchange(value, mesh):
    cfgs, prows, cores = (mesh.shape[axis] for axis in AXES)
    return lax.ppermute(value, AXES, [(d, d ^ 1) for d in range(cfgs * prows * cores)])


def local_eight(mesh, sigma_top, panel_l, diag_inv, pattern):
    f32 = jnp.float32
    half_rows, own_columns = panel_l.shape
    block = sigma_top.shape[0]
    local_sn, width = diag_inv.shape[:2]
    shape = lambda *dims: jax.ShapeDtypeStruct(dims, f32)
    size = 2 * block + SPARE
    panel, square = shape(half_rows, own_columns), shape(half_rows, half_rows)
    children = shape(*diag_inv.shape)
    halves = [jax.ShapeDtypeStruct((half_rows, own_columns), jnp.bfloat16)] * 2
    turned = [jax.ShapeDtypeStruct((own_columns, half_rows), jnp.bfloat16)] * 2
    anywhere = pl.BlockSpec(memory_space=pl.ANY)
    in_hbm = lambda value: pltpu.with_memory_space_constraint(value, pltpu.HBM)
    step = 2 * half_rows * half_rows * own_columns
    mine_a, mine_b, mask = call(
        pieces_kernel,
        [shape(size, block)] * 2 + [shape(local_sn * (half_rows // block), width)],
        40 * step,
        in_hbm(sigma_top),
        in_hbm(pattern),
        specs=[anywhere] * 2,
        scratch=[
            pltpu.VMEM(sigma_top.shape, f32),
            pltpu.SMEM(pattern.shape, jnp.int32),
            pltpu.SemaphoreType.DMA((2,)),
        ],
    )
    got1 = permute(mine_a, mesh, 4, 1)
    got2 = permute(mine_a, mesh, 6, 2)
    got3 = permute(mine_b, mesh, 1, 2)
    got4 = permute(mine_b, mesh, 2, 1)
    got5 = permute(got1, mesh, 1, 2)
    got6 = permute(got4, mesh, 1, 2)
    (got2_again,) = call(again_kernel, [shape(size, block)], 40 * step, got2)
    got7 = permute(got2_again, mesh, 1)
    (got7_again,) = call(again_kernel, [shape(size, block)], 16 * step, got7)
    factor, *own_factor = call(
        factor_kernel,
        [panel, *halves],
        1,
        mask,
        panel_l,
        diag_inv,
    )
    factor_other = exchange(factor, mesh)
    *far_rows, own_part, products, most = call(
        prepare_kernel,
        [*halves, *turned, children, shape(3 * block, own_columns), panel],
        1,
        mine_a, mine_b, got1, got2, got3, got4, factor, factor_other, diag_inv,
    )
    own_half, sent_a, sent_b = call(
        own_half_kernel,
        [square] + [shape(half_rows // 2, own_columns)] * 2,
        36 * step,
        mine_a, got1, got2, got3, got4, got5, got6, products, *far_rows[:2],
    )
    early_a, early_b = exchange(sent_a, mesh), exchange(sent_b, mesh)
    partial, near = call(
        near_kernel,
        [panel, children],
        4 * step,
        own_half, got5, got6, most, *own_factor, factor_other, *far_rows[2:], own_part,
    )
    near_other = exchange(near, mesh)
    late = exchange(got7, mesh)
    far, first = call(
        far_kernel,
        [children, panel],
        1,
        got1, got2, got5, got7_again, early_a, *far_rows,
        scratch=[pltpu.VMEM(square.shape, f32)],
    )
    return tuple(
        call(
            panel_kernel,
            [panel, children],
            1,
            early_a, early_b, late, partial, *far_rows, near, near_other, far, first,
            out_specs=[anywhere] * 2,
            scratch=[
                pltpu.VMEM(square.shape, f32),
                pltpu.VMEM(panel.shape, f32),
                pltpu.VMEM(children.shape, f32),
                pltpu.SemaphoreType.DMA((half_rows // block,)),
                pltpu.SemaphoreType.DMA((local_sn,)),
            ],
        )
    )


def local_any(sigma_top, panel_l, diag_inv, pattern):
    half_rows = panel_l.shape[0]
    local_sn, width = diag_inv.shape[:2]
    row_mask = jnp.repeat(pattern.astype(jnp.float32), W // BLOCK_ROWS, axis=1)
    row_mask = lax.dynamic_slice_in_dim(row_mask, lax.axis_index("pcol") * half_rows, half_rows, 1)
    masked = panel_l.reshape(half_rows, local_sn, width) * jnp.transpose(row_mask)[:, :, None]
    factor = jnp.einsum("wns,nst->wnt", masked, diag_inv, precision=lax.Precision.HIGHEST)
    factor_flat = factor.reshape(half_rows, local_sn * width)
    whole = lax.all_gather(factor_flat, "pcol", axis=0, tiled=True)
    gathered = lax.all_gather(sigma_top, "prow", axis=0, tiled=True)
    sigma = -jnp.einsum("wv,wt->vt", gathered, whole, precision=lax.Precision.HIGHEST)
    sigma_three = sigma.reshape(half_rows, local_sn, width)
    cross = lax.psum(jnp.einsum("wnr,wnt->nrt", factor, sigma_three, precision=lax.Precision.HIGHEST), "pcol")
    own_part = jnp.einsum("nsr,nst->nrt", diag_inv, diag_inv, precision=lax.Precision.HIGHEST)
    return sigma, own_part - cross


def solution(mesh):
    in_specs = (
        P(("cfg", "prow"), "pcol"),
        P(("cfg", "pcol"), "prow"),
        P(("cfg", "prow"), None, None),
        P(("cfg", "prow"), None),
    )
    out_specs = (P(("cfg", "pcol"), "prow"), P(("cfg", "prow"), None, None))
    local = functools.partial(local_eight, mesh) if mesh.shape["prow"] == 8 else local_any
    return jax.shard_map(local, mesh=mesh, in_specs=in_specs, out_specs=out_specs, check_vma=False)
```
